32 devices in a mesh: seq: 2 (over x), ctx: 4 (over z), head: 4 (over y, core).
Axes of the slice: x: 2, y: 2, z: 4, core: 2. Of those that a mesh axis runs over, the one named last changes fastest.
Arguments:
- tokens: bfloat16 [2, 2560, 1024], P('seq', 'ctx'), may hold values from -6 to 6
- doc_lengths: int32 [2, 4], P('seq'), may hold values from 80 to 1920, as said below
- norm_gains: bfloat16 [2, 1024], P(None, 'ctx'), may hold values from 0.5 to 1.5
- w_qkv: bfloat16 [3, 1024, 1024], P(None, 'ctx', 'head'), may hold values from -0.1875 to 0.1875
- w_out: bfloat16 [1024, 1024], P('head', 'ctx'), may hold values from -3 to 3
- w_in: bfloat16 [2, 1024, 2624], P(None, 'ctx', 'head'), may hold values from -0.1875 to 0.1875
- w_down: bfloat16 [2624, 1024], P('head', 'ctx'), may hold values from -0.125 to 0.125
- cotangent: bfloat16 [2, 2560, 1024], P('seq', 'ctx'), may hold values from -6 to 6
Outputs:
- out_tokens: bfloat16 [2, 2560, 1024], P('seq', 'ctx')
- grad_tokens: bfloat16 [2, 2560, 1024], P('seq', 'ctx')
- grad_gains: float32 [2, 1024], P(None, 'ctx')
- grad_qkv: float32 [3, 1024, 1024], P(None, 'ctx', 'head')
- grad_out: float32 [1024, 1024], P('head', 'ctx')
- grad_in: float32 [2, 1024, 2624], P(None, 'ctx', 'head')
- grad_down: float32 [2624, 1024], P('head', 'ctx')
The draws below stay inside these ranges and needn't reach their ends.
Inputs may be any that keep to these rules, and one draw needn't show every extreme that they name: `doc_lengths`: each pack's 4 lengths add up to 2560. In every pack one of them, at a place drawn from the seed, is exactly the stated most, so that this document starts within the first 640 tokens and ends within the last 640; one other, also drawn from the seed, is exactly the stated least.
All inputs are finite; a program needn't handle non-finite values.
Results may differ from the reference program's by a relative error of at most 0.023.
Values may be sent and summed in bfloat16 or wider, within the bound.
A program may use at most 384 MiB of HBM per device.

```python
import math
import jax
import jax.numpy as jnp
from jax import lax

D = 1024
HEADS = 16
HD = 64
FF = 2624
TOK_DEV = 640
DOCS = 4
PACK = 2560
PACKS = 2


def draw_doc_lengths(key, part):
    key = jax.random.fold_in(key, 11)
    weight_key, place_key, zero_key = jax.random.split(key, 3)
    least = max(1, TOK_DEV // 8)
    longest_len = PACK - TOK_DEV
    extra = TOK_DEV - (DOCS - 1) * least
    longest = jax.random.randint(place_key, (PACKS, 1), 0, DOCS, dtype=jnp.int32)
    slots = jnp.arange(DOCS, dtype=jnp.int32)[None, :]
    chosen = slots == longest
    ranks = slots - (slots > longest).astype(jnp.int32)
    zero_rank = jax.random.randint(zero_key, (PACKS, 1), 0, DOCS - 1, dtype=jnp.int32)
    weights = jax.random.randint(weight_key, (PACKS, DOCS), 1, 9, dtype=jnp.int32)
    weights = jnp.where(chosen | (ranks == zero_rank), 0, weights)
    running = jnp.cumsum(weights, axis=1, dtype=jnp.int32)
    total = running[:, -1:]
    upper = extra * running // total
    lower = extra * (running - weights) // total
    others = least + upper - lower
    return jnp.where(chosen, longest_len, others).astype(jnp.int32)


def shard_levels(stream_key, shape, cuts, low, high):
    level, own = 1.0, jax.random.fold_in(stream_key, 6)
    for dim, shards_of in cuts:
        steps = jnp.exp(jax.random.uniform(jax.random.fold_in(own, dim), (shards_of,), jnp.float32, low / len(cuts), high / len(cuts)))
        level = level * jnp.repeat(steps, shape[dim] // shards_of).reshape([-1 if axis == dim else 1 for axis in range(len(shape))])
    return level


def noise(own_key, shape, spread, bound, cuts=(), kind=jnp.bfloat16):
    entries = spread * jax.random.normal(own_key, shape, jnp.float32)
    if cuts:
        entries = entries * shard_levels(own_key, shape, cuts, -0.22, 0.18)
    return jnp.clip(entries, -bound, bound).astype(kind)


def setup_inputs(seed: int = 0) -> dict:
    key_list = jax.random.split(jax.random.key(seed), 9)
    tokens = noise(key_list[0], (PACKS, PACK, D), 1.0, 6.0, ((0, 2), (1, 4)))
    doc_lengths = draw_doc_lengths(jax.random.fold_in(key_list[8], 71), 0)
    norm_gains = jnp.clip(1.0 + 0.1 * jax.random.normal(key_list[2], (2, D), jnp.float32), 0.5, 1.5).astype(jnp.bfloat16)
    w_qkv = noise(key_list[3], (3, D, HEADS * HD), D ** -0.5, 0.1875, ((1, 4), (2, 4)))
    w_out = noise(key_list[4], (HEADS * HD, D), (PACK ** 0.5 * 0.01), 3.0, ((0, 4), (1, 4)))
    w_in = noise(key_list[5], (2, D, FF), D ** -0.5, 0.1875, ((1, 4), (2, 4)))
    w_down = noise(key_list[6], (FF, D), FF ** -0.5, 0.125, ((0, 4), (1, 4)))
    cotangent = noise(key_list[7], (PACKS, PACK, D), 1.0, 6.0, ((0, 2), (1, 4)))
    return {"tokens": tokens, "doc_lengths": doc_lengths, "norm_gains": norm_gains, "w_qkv": w_qkv, "w_out": w_out, "w_in": w_in, "w_down": w_down, "cotangent": cotangent}


norm_eps = 1e-05
theta_base = 160000.0
masked_score = -1e+30
highest = lax.Precision.HIGHEST

@jax.custom_vjp
def low(v):
    return lax.optimization_barrier(v.astype(jnp.bfloat16)).astype(jnp.float32)

@jax.custom_vjp
def low_back(v):
    return v

def low_keep(v):
    return (low(v), None)

def low_pass(kept, grad):
    return (grad,)

def back_keep(v):
    return (v, None)

def back_low(kept, grad):
    return (low(grad),)
low.defvjp(low_keep, low_pass)
low_back.defvjp(back_keep, back_low)

def token_layout(lengths, first_row, row_count):
    doc_ends = jnp.cumsum(lengths, dtype=jnp.int32)
    places = first_row + jnp.arange(row_count, dtype=jnp.int32)
    passed = places[:, None] >= doc_ends[None, :]
    doc_index = lax.optimization_barrier(jnp.sum(passed.astype(jnp.int32), axis=1, dtype=jnp.int32))
    starts = lax.optimization_barrier(jnp.sum(jnp.where(passed, lengths[None, :], 0), axis=1, dtype=jnp.int32))
    return (doc_index, places - starts)

def rotate(values, positions, turn_sign):
    leading = values.shape[:-1]
    head_count = values.shape[-1] // HD
    half_width = HD // 2
    frequency = theta_base ** (-(jnp.arange(half_width, dtype=jnp.float32) * (2.0 / HD)))
    angles = positions.astype(jnp.float32)[..., None] * frequency
    cosine = jnp.cos(angles)[..., None, :]
    sine_part = turn_sign * jnp.sin(angles)[..., None, :]
    shaped = values.reshape(leading + (head_count, HD))
    lower_half = shaped[..., :half_width]
    upper_half = shaped[..., half_width:]
    turned = jnp.concatenate([lower_half * cosine - upper_half * sine_part, upper_half * cosine + lower_half * sine_part], axis=-1)
    return turned.reshape(values.shape)

def layer_norm(values, gain_row):
    mean_value = lax.optimization_barrier(jnp.mean(values, axis=-1, keepdims=True))
    centered = values - mean_value
    variance = lax.optimization_barrier(jnp.mean(centered * centered, axis=-1, keepdims=True))
    inverse = lax.rsqrt(variance + norm_eps)
    normed = centered * inverse
    return (normed, inverse, normed * gain_row)

def exact_gelu(values):
    return jax.nn.gelu(values, approximate=False)

def attend_block(query_block, block_doc, key_rows, value_rows, key_doc):
    scores = low_back(jnp.einsum('qhd,khd->hqk', query_block, key_rows, precision=highest))
    allowed = (block_doc[:, None] == key_doc[None, :])[None]
    scores = jnp.where(allowed, scores, masked_score)
    top_score = lax.optimization_barrier(jnp.max(scores, axis=2, keepdims=True))
    weights = jnp.where(allowed, jnp.exp(scores - top_score), 0.0)
    running_sum = lax.optimization_barrier(jnp.sum(weights, axis=2))
    weighted = jnp.einsum('hqk,khd->qhd', low(weights), value_rows, precision=highest)
    return weighted / running_sum.T[:, :, None]

def attend_pack(pieces):
    query_rows, key_rows, value_rows, doc_row = pieces
    block_rows = math.gcd(PACK, 512)
    block_count = PACK // block_rows
    query_blocks = query_rows.reshape(block_count, block_rows, HEADS, HD)
    doc_blocks = doc_row.reshape(block_count, block_rows)
    checked = jax.checkpoint(attend_block)
    outputs = lax.map(lambda block_pair: checked(block_pair[0], block_pair[1], key_rows, value_rows, doc_row), (query_blocks, doc_blocks))
    return outputs.reshape(PACK, HEADS * HD)

def reference(tokens, doc_lengths, norm_gains, w_qkv, w_out, w_in, w_down, cotangent):
    doc_index, positions = jax.vmap(lambda row_lengths: token_layout(row_lengths, 0, PACK))(doc_lengths)

    def forward(hidden, gains, qkv_weight, out_weight, in_weight, down_weight):
        input_one = low(layer_norm(hidden, gains[0])[2])
        raw_proj = low_back(jnp.einsum('std,cdn->stcn', input_one, qkv_weight, precision=highest))
        queries = low(rotate(raw_proj[:, :, 0], positions, 1.0) * HD ** (-0.5))
        key_rows = low(rotate(raw_proj[:, :, 1], positions, 1.0))
        value_rows = low(raw_proj[:, :, 2])
        shape_heads = (PACKS, PACK, HEADS, HD)
        attn_float = lax.map(attend_pack, (queries.reshape(shape_heads), key_rows.reshape(shape_heads), value_rows.reshape(shape_heads), doc_index))
        attn_low = low(low_back(attn_float))
        branch_one = low_back(jnp.einsum('stn,nd->std', attn_low, out_weight, precision=highest))
        resid_one = hidden + branch_one
        input_two = low(layer_norm(resid_one, gains[1])[2])
        gate_up = low_back(jnp.einsum('std,cdf->stcf', input_two, in_weight, precision=highest))
        mixed_low = low(exact_gelu(gate_up[:, :, 0]) * gate_up[:, :, 1])
        return resid_one + jnp.einsum('stf,fd->std', mixed_low, down_weight, precision=highest)
    result, pullback = jax.vjp(forward, tokens.astype(jnp.float32), norm_gains.astype(jnp.float32), w_qkv.astype(jnp.float32), w_out.astype(jnp.float32), w_in.astype(jnp.float32), w_down.astype(jnp.float32))
    gradients = pullback(cotangent.astype(jnp.float32))
    return (result.astype(jnp.bfloat16), gradients[0].astype(jnp.bfloat16), gradients[1], gradients[2], gradients[3], gradients[4], gradients[5])
```

```python
import jax
import jax.numpy as jnp
from jax import lax
from jax.sharding import PartitionSpec as P

HD = 64


norm_eps = 1e-05
theta_base = 160000.0
masked_score = -1e30


def passed_along(block, axis, distance):
    devices = range(lax.axis_size(axis))
    route = [((i - distance) % len(devices), i) for i in devices]
    return lax.ppermute(block, axis, route)


def token_layout(lengths, first_row, row_count):
    doc_ends = jnp.cumsum(lengths, dtype=jnp.int32)
    places = first_row + jnp.arange(row_count, dtype=jnp.int32)
    passed = places[:, None] >= doc_ends[None, :]
    doc_index = jnp.sum(passed.astype(jnp.int32), axis=1, dtype=jnp.int32)
    starts = jnp.sum(jnp.where(passed, lengths[None, :], 0), axis=1, dtype=jnp.int32)
    return (doc_index, places - starts)


def rotate(values, positions, turn_sign):
    leading = values.shape[:-1]
    head_count = values.shape[-1] // HD
    half_width = HD // 2
    frequency = theta_base ** (-(jnp.arange(half_width, dtype=jnp.float32) * (2.0 / HD)))
    angles = positions.astype(jnp.float32)[..., None] * frequency
    cosine = jnp.cos(angles)[..., None, :]
    sine_part = turn_sign * jnp.sin(angles)[..., None, :]
    shaped = values.reshape(leading + (head_count, HD))
    lower_half = shaped[..., :half_width]
    upper_half = shaped[..., half_width:]
    turned = jnp.concatenate(
        [
            lower_half * cosine - upper_half * sine_part,
            upper_half * cosine + lower_half * sine_part,
        ],
        axis=-1,
    )
    return turned.reshape(values.shape)


def layer_norm(values, gain_row):
    mean_value = jnp.mean(values, axis=-1, keepdims=True)
    centered = values - mean_value
    variance = jnp.mean(centered * centered, axis=-1, keepdims=True)
    inverse = lax.rsqrt(variance + norm_eps)
    normed = centered * inverse
    return (normed, inverse, normed * gain_row)


def norm_back(grad_scaled, normed, inverse, gain_row):
    grad_normed = grad_scaled * gain_row
    mean_grad = jnp.mean(grad_normed, axis=-1, keepdims=True)
    mean_proj = jnp.mean(grad_normed * normed, axis=-1, keepdims=True)
    grad_values = inverse * (grad_normed - mean_grad - normed * mean_proj)
    return (grad_values, jnp.sum(grad_scaled * normed, axis=0))


def exact_gelu(values):
    return jax.nn.gelu(values, approximate=False)


def back_step(
    query_part, grad_part, lse_part, delta_part, query_doc, key_part, value_part, key_doc
):
    head_count = query_part.shape[1] // HD
    query_heads = query_part.reshape(query_part.shape[0], head_count, HD)
    grad_heads = grad_part.reshape(grad_part.shape[0], head_count, HD)
    key_heads = key_part.reshape(key_part.shape[0], head_count, HD)
    value_heads = value_part.reshape(value_part.shape[0], head_count, HD)
    allowed = (query_doc[:, None] == key_doc[None, :])[None]
    scores = jnp.einsum("qhd,khd->hqk", query_heads, key_heads, preferred_element_type=jnp.float32)
    prob_rows = jnp.where(allowed, jnp.exp(scores - lse_part[:, :, None]), 0.0)
    grad_value = jnp.einsum(
        "hqk,qhd->khd",
        prob_rows.astype(jnp.bfloat16),
        grad_heads,
        preferred_element_type=jnp.float32,
    )
    grad_probs = jnp.einsum(
        "qhd,khd->hqk", grad_heads, value_heads, preferred_element_type=jnp.float32
    )
    grad_scores = (prob_rows * (grad_probs - delta_part[:, :, None])).astype(jnp.bfloat16)
    grad_query = jnp.einsum(
        "hqk,khd->qhd", grad_scores, key_heads, preferred_element_type=jnp.float32
    )
    grad_key = jnp.einsum(
        "hqk,qhd->khd", grad_scores, query_heads, preferred_element_type=jnp.float32
    )
    return (
        grad_query.reshape(query_part.shape[0], -1),
        grad_key.reshape(key_part.shape[0], -1),
        grad_value.reshape(key_part.shape[0], -1),
    )


def per_device_ring(tokens, doc_lengths, norm_gains, w_qkv, w_out, w_in, w_down, cotangent):
    row_count = tokens.shape[1]
    hidden = tokens[0].astype(jnp.float32)
    lengths = doc_lengths[0]
    group_size = lax.axis_size("ctx")
    my_index = lax.axis_index("ctx")
    doc_here, pos_here = token_layout(lengths, my_index * row_count, row_count)
    gains_full, qkv_full, out_full, in_full, down_full = (
        lax.all_gather(norm_gains, "ctx", axis=1, tiled=True),
        lax.all_gather(w_qkv, "ctx", axis=1, tiled=True),
        lax.all_gather(w_out, "ctx", axis=1, tiled=True),
        lax.all_gather(w_in, "ctx", axis=1, tiled=True),
        lax.all_gather(w_down, "ctx", axis=1, tiled=True),
    )
    gains_float = gains_full.astype(jnp.float32)
    normed_one, inverse_one, scaled_one = layer_norm(hidden, gains_float[0])
    input_one = scaled_one.astype(jnp.bfloat16)
    raw_proj = jnp.einsum("td,cdn->tcn", input_one, qkv_full, preferred_element_type=jnp.float32)
    proj_width = raw_proj.shape[2]
    head_count = proj_width // HD
    scale_value = HD ** (-0.5)
    queries = (rotate(raw_proj[:, 0], pos_here, 1.0) * scale_value).astype(jnp.bfloat16)
    key_rows = rotate(raw_proj[:, 1], pos_here, 1.0).astype(jnp.bfloat16)
    value_rows = raw_proj[:, 2].astype(jnp.bfloat16)
    query_heads = queries.reshape(row_count, head_count, HD)
    top_score = jnp.full((head_count, row_count), masked_score, jnp.float32)
    weighted = jnp.zeros((row_count, proj_width), jnp.float32)
    key_piece = lax.all_gather(key_rows, "ctx", axis=0, tiled=True)
    value_piece = lax.all_gather(value_rows, "ctx", axis=0, tiled=True)
    piece_rows = key_piece.shape[0]
    key_doc, unused_pos = token_layout(lengths, jnp.int32(0), piece_rows)
    allowed = (doc_here[:, None] == key_doc[None, :])[None]
    scores = jnp.einsum(
        "qhd,khd->hqk",
        query_heads,
        key_piece.reshape(piece_rows, head_count, HD),
        preferred_element_type=jnp.float32,
    )
    scores = jnp.where(allowed, scores, masked_score)
    new_top = jnp.maximum(top_score, jnp.max(scores, axis=2))
    weights = jnp.where(allowed, jnp.exp(scores - new_top[:, :, None]), 0.0)
    factor = jnp.exp(top_score - new_top)
    running_sum = jnp.sum(weights, axis=2)
    update = jnp.einsum(
        "hqk,khd->qhd",
        weights.astype(jnp.bfloat16),
        value_piece.reshape(piece_rows, head_count, HD),
        preferred_element_type=jnp.float32,
    )
    weighted = weighted.reshape(row_count, head_count, HD) * factor.T[:, :, None] + update
    top_score, running_sum, weighted = (
        new_top,
        running_sum,
        weighted.reshape(row_count, proj_width),
    )
    log_total = top_score + jnp.log(running_sum)
    attn_float = (weighted.reshape(row_count, head_count, HD) / running_sum.T[:, :, None]).reshape(
        row_count, proj_width
    )
    attn_low = attn_float.astype(jnp.bfloat16)
    partial_out = jnp.dot(attn_low, out_full, preferred_element_type=jnp.float32)
    branch_one = lax.psum(partial_out.astype(jnp.bfloat16), "head").astype(jnp.float32)
    resid_one = hidden + branch_one
    normed_two, inverse_two, scaled_two = layer_norm(resid_one, gains_float[1])
    input_two = scaled_two.astype(jnp.bfloat16)
    gate_up = jnp.einsum("td,cdf->tcf", input_two, in_full, preferred_element_type=jnp.float32)
    activated, gelu_back = jax.vjp(exact_gelu, gate_up[:, 0])
    mixed_low = (activated * gate_up[:, 1]).astype(jnp.bfloat16)
    partial_ffn = jnp.dot(mixed_low, down_full, preferred_element_type=jnp.float32)
    branch_two = lax.psum(partial_ffn.astype(jnp.bfloat16), "head").astype(jnp.float32)
    result = (resid_one + branch_two).astype(jnp.bfloat16)
    gains_back, qkv_back, out_back, in_back, down_back = (
        gains_float,
        qkv_full,
        out_full,
        in_full,
        down_full,
    )
    grad_rows = cotangent[0]
    grad_down = jnp.einsum("tf,td->fd", mixed_low, grad_rows, preferred_element_type=jnp.float32)
    grad_mixed = jnp.einsum("td,fd->tf", grad_rows, down_back, preferred_element_type=jnp.float32)
    grad_gate = gelu_back(grad_mixed * gate_up[:, 1])[0]
    grad_up = grad_mixed * activated
    grad_gate_up = jnp.stack([grad_gate, grad_up], axis=1).astype(jnp.bfloat16)
    grad_in = jnp.einsum("td,tcf->cdf", input_two, grad_gate_up, preferred_element_type=jnp.float32)
    partial_two = jnp.einsum(
        "tcf,cdf->td", grad_gate_up, in_back, preferred_element_type=jnp.float32
    )
    grad_input_two = lax.psum(partial_two.astype(jnp.bfloat16), "head").astype(jnp.float32)
    grad_norm_two, gain_grad_two = norm_back(grad_input_two, normed_two, inverse_two, gains_back[1])
    grad_resid = grad_rows.astype(jnp.float32) + grad_norm_two
    grad_branch = grad_resid.astype(jnp.bfloat16)
    grad_out = jnp.einsum("tn,td->nd", attn_low, grad_branch, preferred_element_type=jnp.float32)
    grad_attn = jnp.einsum(
        "td,nd->tn", grad_branch, out_back, preferred_element_type=jnp.float32
    ).astype(jnp.bfloat16)
    delta_rows = jnp.sum(
        (grad_attn.astype(jnp.float32) * attn_float).reshape(row_count, head_count, HD), axis=2
    ).T
    zero_rows = jnp.zeros((row_count, proj_width), jnp.float32)

    def key_work(step_index, key_block, value_block, key_grad, value_grad, query_grad):
        anchor = (my_index - step_index) % group_size
        key_doc, unused_pos = token_layout(lengths, anchor * row_count, row_count)
        step_grads = back_step(
            queries, grad_attn, log_total, delta_rows, doc_here, key_block, value_block, key_doc
        )
        return (key_grad + step_grads[1], value_grad + step_grads[2], query_grad + step_grads[0])

    def send_key_grads(key_grad, value_grad):
        return (
            passed_along(key_grad.astype(jnp.bfloat16), "ctx", 1).astype(key_grad.dtype),
            passed_along(value_grad.astype(jnp.bfloat16), "ctx", 1).astype(value_grad.dtype),
        )

    def key_turn(step_index, state_now):
        key_block, value_block, key_grad, value_grad, query_grad = state_now
        key_grad, value_grad, query_grad = key_work(
            step_index, key_block, value_block, key_grad, value_grad, query_grad
        )
        key_block, value_block = passed_along((key_block, value_block), "ctx", 1)
        key_grad, value_grad = send_key_grads(key_grad, value_grad)
        return (key_block, value_block, key_grad, value_grad, query_grad)

    state_now = lax.fori_loop(
        0, group_size - 1, key_turn, (key_rows, value_rows, zero_rows, zero_rows, zero_rows)
    )
    last_grads = key_work(
        group_size - 1, state_now[0], state_now[1], state_now[2], state_now[3], state_now[4]
    )
    grad_query = last_grads[2]
    grad_key, grad_value = send_key_grads(last_grads[0], last_grads[1])
    grad_query_pre = rotate(grad_query, pos_here, -1.0) * scale_value
    grad_key_pre = rotate(grad_key, pos_here, -1.0)
    grad_raw = jnp.stack([grad_query_pre, grad_key_pre, grad_value], axis=1).astype(jnp.bfloat16)
    grad_qkv = jnp.einsum("td,tcn->cdn", input_one, grad_raw, preferred_element_type=jnp.float32)
    partial_one = jnp.einsum("tcn,cdn->td", grad_raw, qkv_back, preferred_element_type=jnp.float32)
    grad_input_one = lax.psum(partial_one.astype(jnp.bfloat16), "head").astype(jnp.float32)
    grad_norm_one, gain_grad_one = norm_back(grad_input_one, normed_one, inverse_one, gains_back[0])
    grad_tokens = (grad_resid + grad_norm_one).astype(jnp.bfloat16)
    grad_gains = jnp.stack([gain_grad_one, gain_grad_two])
    share_gains, share_qkv, share_out, share_in, share_down = (
        lax.psum_scatter(
            grad_gains.astype(jnp.bfloat16), "ctx", scatter_dimension=1, tiled=True
        ).astype(jnp.float32),
        lax.psum_scatter(
            grad_qkv.astype(jnp.bfloat16), "ctx", scatter_dimension=1, tiled=True
        ).astype(jnp.float32),
        lax.psum_scatter(
            grad_out.astype(jnp.bfloat16), "ctx", scatter_dimension=1, tiled=True
        ).astype(jnp.float32),
        lax.psum_scatter(
            grad_in.astype(jnp.bfloat16), "ctx", scatter_dimension=1, tiled=True
        ).astype(jnp.float32),
        lax.psum_scatter(
            grad_down.astype(jnp.bfloat16), "ctx", scatter_dimension=1, tiled=True
        ).astype(jnp.float32),
    )
    total_gains, total_qkv, total_out, total_in, total_down = (
        lax.psum(share_gains.astype(jnp.bfloat16), "seq").astype(jnp.float32),
        lax.psum(share_qkv.astype(jnp.bfloat16), "seq").astype(jnp.float32),
        lax.psum(share_out.astype(jnp.bfloat16), "seq").astype(jnp.float32),
        lax.psum(share_in.astype(jnp.bfloat16), "seq").astype(jnp.float32),
        lax.psum(share_down.astype(jnp.bfloat16), "seq").astype(jnp.float32),
    )
    return (
        result[None],
        grad_tokens[None],
        total_gains,
        total_qkv,
        total_out,
        total_in,
        total_down,
    )


def pair_swap(block, axis, mask):
    size = lax.axis_size(axis)
    return lax.ppermute(block, axis, [(i, i ^ mask) for i in range(size)])


def gather_weight(weight, dim):
    half = weight.shape[dim] // lax.axis_size("seq")
    mine = lax.dynamic_slice_in_dim(weight, lax.axis_index("seq") * half, half, dim)
    return lax.all_gather(mine, ("ctx", "seq"), axis=dim, tiled=True)


def gather_gains(gains):
    group = lax.axis_size("ctx")
    if group > 4:
        return lax.all_gather(gains, "ctx", axis=1, tiled=True)
    me = lax.axis_index("ctx")
    width = gains.shape[1]
    full = jnp.zeros((gains.shape[0], width * group), gains.dtype)
    for k in range(group):
        block = gains if k == 0 else passed_along(gains, "ctx", k)
        full = lax.dynamic_update_slice_in_dim(full, block, ((me - k) % group) * width, 1)
    return full


def reduce_weight(grad):
    return lax.psum_scatter(grad, ("ctx", "seq"), scatter_dimension=1, tiled=True)


def reduce_weight_rows(share):
    other = pair_swap(share, "seq", 1)
    first = lax.axis_index("seq") == 0
    low_part = jnp.where(first, share, other)
    high_part = jnp.where(first, other, share)
    return jnp.concatenate([low_part, high_part], axis=1).astype(jnp.float32)


def reduce_gains(grads):
    group = lax.axis_size("ctx")
    me = lax.axis_index("ctx")
    width = grads.shape[1] // group
    if group > 4:
        share = lax.psum_scatter(grads, "ctx", scatter_dimension=1, tiled=True)
    else:
        share = lax.dynamic_slice_in_dim(grads, me * width, width, 1)
        for k in range(1, group):
            block = lax.dynamic_slice_in_dim(grads, ((me + k) % group) * width, width, 1)
            share = share + passed_along(block, "ctx", k)
    return share + pair_swap(share, "seq", 1)


def head_sum(partial):
    half = partial.shape[0] // 2
    core = lax.axis_index("head") % 2
    mine = lax.dynamic_slice_in_dim(partial, core * half, half, 0)
    theirs = lax.dynamic_slice_in_dim(partial, (1 - core) * half, half, 0).astype(jnp.bfloat16)
    pair = (mine + pair_swap(theirs, "head", 1).astype(jnp.float32)).astype(jnp.bfloat16)
    far = pair_swap(pair, "head", 2)
    total = (pair.astype(jnp.float32) + far.astype(jnp.float32)).astype(jnp.bfloat16)
    other = pair_swap(total, "head", 1)
    first = core == 0
    return jnp.concatenate(
        [jnp.where(first, total, other), jnp.where(first, other, total)], axis=0
    ).astype(jnp.float32)


def swap_blocks(blocks, sign):
    group = lax.axis_size("ctx")
    me = lax.axis_index("ctx")
    got = [lax.dynamic_index_in_dim(blocks, me, 0, keepdims=False)]
    for k in range(1, group):
        send = lax.dynamic_index_in_dim(blocks, (me + k) % group, 0, keepdims=False)
        got.append(passed_along(send, "ctx", k))
    stacked = jnp.stack(got)
    return [
        lax.dynamic_index_in_dim(stacked, (me - j) % group, 0, keepdims=False)
        for j in range(group)
    ]


def turn(values, cosine, sine):
    half = HD // 2
    lower, upper = values[..., :half, :], values[..., half:, :]
    return jnp.concatenate(
        [lower * cosine - upper * sine, upper * cosine + lower * sine], axis=-2
    )


def tables(positions):
    frequency = theta_base ** (-(jnp.arange(HD // 2, dtype=jnp.float32) * (2.0 / HD)))
    angles = frequency[:, None] * positions.astype(jnp.float32)[None, :]
    return (jnp.cos(angles), jnp.sin(angles))


def attend(q, k, v, doc):
    allowed = (doc[:, None] == doc[None, :])[None]
    scores = jnp.einsum("ndi,ndj->nij", q, k, preferred_element_type=jnp.float32)
    scores = jnp.where(allowed, scores, masked_score)
    top = jnp.max(scores, axis=2)
    weights = jnp.where(allowed, jnp.exp(scores - top[:, :, None]), 0.0)
    total = jnp.sum(weights, axis=2)
    out = jnp.einsum(
        "ndj,nij->ndi", v, weights.astype(jnp.bfloat16), preferred_element_type=jnp.float32
    )
    return (out / total[:, None, :], top + jnp.log(total))


def attend_back(q, k, v, doc, lse, out, grad):
    allowed = (doc[:, None] == doc[None, :])[None]
    delta = jnp.sum(grad.astype(jnp.float32) * out, axis=1)
    scores = jnp.einsum("ndi,ndj->nij", q, k, preferred_element_type=jnp.float32)
    probs = jnp.where(allowed, jnp.exp(scores - lse[:, :, None]), 0.0)
    grad_v = jnp.einsum(
        "ndi,nij->ndj", grad, probs.astype(jnp.bfloat16), preferred_element_type=jnp.float32
    )
    grad_probs = jnp.einsum("ndi,ndj->nij", grad, v, preferred_element_type=jnp.float32)
    grad_s = (probs * (grad_probs - delta[:, :, None])).astype(jnp.bfloat16)
    grad_q = jnp.einsum("ndj,nij->ndi", k, grad_s, preferred_element_type=jnp.float32)
    grad_k = jnp.einsum("ndi,nij->ndj", q, grad_s, preferred_element_type=jnp.float32)
    return (grad_q, grad_k, grad_v)


def per_device(tokens, doc_lengths, norm_gains, w_qkv, w_out, w_in, w_down, cotangent):
    rows = tokens.shape[1]
    hidden = tokens[0].astype(jnp.float32)
    lengths = doc_lengths[0]
    group = lax.axis_size("ctx")
    me = lax.axis_index("ctx")
    width = w_qkv.shape[2]
    heads = width // HD
    each = heads // group
    scale = HD ** (-0.5)
    gains = gather_gains(norm_gains).astype(jnp.float32)
    qkv_full = gather_weight(w_qkv, 1)
    out_full = gather_weight(w_out, 1)
    in_full = gather_weight(w_in, 1)
    down_full = gather_weight(w_down, 1)
    doc_all, pos_all = token_layout(lengths, jnp.int32(0), rows * group)
    cos_all, sin_all = tables(pos_all)
    cos_here = lax.dynamic_slice_in_dim(cos_all, me * rows, rows, 1)
    sin_here = lax.dynamic_slice_in_dim(sin_all, me * rows, rows, 1)

    normed_one, inverse_one, scaled_one = layer_norm(hidden, gains[0])
    input_one = scaled_one.astype(jnp.bfloat16)
    raw = jnp.einsum("cdn,td->cnt", qkv_full, input_one, preferred_element_type=jnp.float32)
    raw = raw.reshape(3, heads, HD, rows)
    q = (turn(raw[0], cos_here, sin_here) * scale).astype(jnp.bfloat16)
    k = turn(raw[1], cos_here, sin_here).astype(jnp.bfloat16)
    v = raw[2].astype(jnp.bfloat16)
    blocks = jnp.stack([q, k, v], axis=1).reshape(group, each, 3, HD, rows)
    mine = jnp.concatenate(swap_blocks(blocks, 1), axis=-1)
    q, k, v = (mine[:, 0], mine[:, 1], mine[:, 2])
    attn_float, lse = attend(q, k, v, doc_all)
    parts = attn_float.astype(jnp.bfloat16).reshape(each, HD, group, rows).transpose(2, 0, 1, 3)
    attn_low = jnp.concatenate(swap_blocks(parts, -1), axis=0).reshape(width, rows)

    partial_out = jnp.einsum("nt,nd->td", attn_low, out_full, preferred_element_type=jnp.float32)
    resid_one = hidden + head_sum(partial_out)
    normed_two, inverse_two, scaled_two = layer_norm(resid_one, gains[1])
    input_two = scaled_two.astype(jnp.bfloat16)
    gate_up = jnp.einsum("td,cdf->tcf", input_two, in_full, preferred_element_type=jnp.float32)
    activated, gelu_back = jax.vjp(exact_gelu, gate_up[:, 0])
    mixed_low = (activated * gate_up[:, 1]).astype(jnp.bfloat16)
    partial_ffn = jnp.dot(mixed_low, down_full, preferred_element_type=jnp.float32)

    grad_rows = cotangent[0]
    grad_mixed = jnp.einsum("td,fd->tf", grad_rows, down_full, preferred_element_type=jnp.float32)
    grad_gate = gelu_back(grad_mixed * gate_up[:, 1])[0]
    grad_up = grad_mixed * activated
    grad_gate_up = jnp.stack([grad_gate, grad_up], axis=1).astype(jnp.bfloat16)
    partial_two = jnp.einsum(
        "tcf,cdf->td", grad_gate_up, in_full, preferred_element_type=jnp.float32
    )
    grad_input_two = head_sum(partial_two)
    grad_down = jnp.einsum(
        "tf,td->fd", mixed_low, grad_rows, preferred_element_type=jnp.float32
    ).astype(jnp.bfloat16)
    grad_in = jnp.einsum(
        "td,tcf->cdf", input_two, grad_gate_up, preferred_element_type=jnp.float32
    ).astype(jnp.bfloat16)
    grad_input_two, grad_down, grad_in = lax.optimization_barrier(
        (grad_input_two, grad_down, grad_in)
    )
    share_down = reduce_weight(grad_down)
    share_in = reduce_weight(grad_in)
    result = (resid_one + head_sum(partial_ffn)).astype(jnp.bfloat16)
    grad_norm_two, gain_grad_two = norm_back(grad_input_two, normed_two, inverse_two, gains[1])
    grad_resid = grad_rows.astype(jnp.float32) + grad_norm_two
    grad_branch = grad_resid.astype(jnp.bfloat16)
    grad_attn = jnp.einsum(
        "nd,td->nt", out_full, grad_branch, preferred_element_type=jnp.float32
    ).astype(jnp.bfloat16)
    grad_mine = jnp.concatenate(
        swap_blocks(grad_attn.reshape(group, each, HD, rows), 1), axis=-1
    )
    grad_out = jnp.einsum(
        "nt,td->nd", attn_low, grad_branch, preferred_element_type=jnp.float32
    ).astype(jnp.bfloat16)
    grad_mine, grad_out = lax.optimization_barrier((grad_mine, grad_out))
    share_out = reduce_weight(grad_out)
    grad_q, grad_k, grad_v = attend_back(q, k, v, doc_all, lse, attn_float, grad_mine)
    grad_q = turn(grad_q, cos_all, -sin_all) * scale
    grad_k = turn(grad_k, cos_all, -sin_all)
    back = jnp.stack([grad_q, grad_k, grad_v], axis=1).astype(jnp.bfloat16)
    back = back.reshape(each, 3, HD, group, rows).transpose(3, 0, 1, 2, 4)
    grad_raw = jnp.concatenate(swap_blocks(back, -1), axis=0)
    grad_raw = grad_raw.transpose(1, 0, 2, 3).reshape(3, width, rows)
    partial_one = jnp.einsum(
        "cnt,cdn->td", grad_raw, qkv_full, preferred_element_type=jnp.float32
    )
    grad_qkv = jnp.einsum(
        "td,cnt->cdn", input_one, grad_raw, preferred_element_type=jnp.float32
    ).astype(jnp.bfloat16)
    partial_one, grad_qkv, share_down, share_in, share_out = lax.optimization_barrier(
        (partial_one, grad_qkv, share_down, share_in, share_out)
    )
    share_qkv = reduce_weight(grad_qkv)
    grad_input_one = head_sum(partial_one)
    grad_norm_one, gain_grad_one = norm_back(grad_input_one, normed_one, inverse_one, gains[0])
    grad_tokens = (grad_resid + grad_norm_one).astype(jnp.bfloat16)
    total_gains = reduce_gains(jnp.stack([gain_grad_one, gain_grad_two]))
    return (
        result[None],
        grad_tokens[None],
        total_gains,
        reduce_weight_rows(share_qkv),
        reduce_weight_rows(share_out),
        reduce_weight_rows(share_in),
        reduce_weight_rows(share_down),
    )


def solution(mesh):
    heads = 1024 // HD // mesh.shape["head"]
    body = per_device if heads % mesh.shape["ctx"] == 0 else per_device_ring
    return jax.shard_map(
        body,
        mesh=mesh,
        in_specs=(
            P("seq", "ctx", None),
            P("seq", None),
            P(None, "ctx"),
            P(None, "ctx", "head"),
            P("head", "ctx"),
            P(None, "ctx", "head"),
            P("head", "ctx"),
            P("seq", "ctx", None),
        ),
        out_specs=(
            P("seq", "ctx", None),
            P("seq", "ctx", None),
            P(None, "ctx"),
            P(None, "ctx", "head"),
            P("head", "ctx"),
            P(None, "ctx", "head"),
            P("head", "ctx"),
        ),
        check_vma=False,
    )
```

```python
import functools
import jax
import jax.numpy as jnp
from jax import lax
from jax.experimental import pallas as pl
from jax.experimental.pallas import tpu as pltpu
from jax.sharding import PartitionSpec as P

HD = 64


norm_eps = 1e-05
theta_base = 160000.0
masked_score = -1e30


def passed_along(block, axis, distance):
    devices = range(lax.axis_size(axis))
    route = [((i - distance) % len(devices), i) for i in devices]
    return lax.ppermute(block, axis, route)


def token_layout(lengths, first_row, row_count):
    doc_ends = jnp.cumsum(lengths, dtype=jnp.int32)
    places = first_row + jnp.arange(row_count, dtype=jnp.int32)
    passed = places[:, None] >= doc_ends[None, :]
    doc_index = jnp.sum(passed.astype(jnp.int32), axis=1, dtype=jnp.int32)
    starts = jnp.sum(jnp.where(passed, lengths[None, :], 0), axis=1, dtype=jnp.int32)
    return (doc_index, places - starts)


def rotate(values, positions, turn_sign):
    leading = values.shape[:-1]
    head_count = values.shape[-1] // HD
    half_width = HD // 2
    frequency = theta_base ** (-(jnp.arange(half_width, dtype=jnp.float32) * (2.0 / HD)))
    angles = positions.astype(jnp.float32)[..., None] * frequency
    cosine = jnp.cos(angles)[..., None, :]
    sine_part = turn_sign * jnp.sin(angles)[..., None, :]
    shaped = values.reshape(leading + (head_count, HD))
    lower_half = shaped[..., :half_width]
    upper_half = shaped[..., half_width:]
    turned = jnp.concatenate(
        [
            lower_half * cosine - upper_half * sine_part,
            upper_half * cosine + lower_half * sine_part,
        ],
        axis=-1,
    )
    return turned.reshape(values.shape)


def layer_norm(values, gain_row):
    mean_value = jnp.mean(values, axis=-1, keepdims=True)
    centered = values - mean_value
    variance = jnp.mean(centered * centered, axis=-1, keepdims=True)
    inverse = lax.rsqrt(variance + norm_eps)
    normed = centered * inverse
    return (normed, inverse, normed * gain_row)


def norm_back(grad_scaled, normed, inverse, gain_row):
    grad_normed = grad_scaled * gain_row
    mean_grad = jnp.mean(grad_normed, axis=-1, keepdims=True)
    mean_proj = jnp.mean(grad_normed * normed, axis=-1, keepdims=True)
    grad_values = inverse * (grad_normed - mean_grad - normed * mean_proj)
    return (grad_values, jnp.sum(grad_scaled * normed, axis=0))


def exact_gelu(values):
    return jax.nn.gelu(values, approximate=False)


def back_step(
    query_part, grad_part, lse_part, delta_part, query_doc, key_part, value_part, key_doc
):
    head_count = query_part.shape[1] // HD
    query_heads = query_part.reshape(query_part.shape[0], head_count, HD)
    grad_heads = grad_part.reshape(grad_part.shape[0], head_count, HD)
    key_heads = key_part.reshape(key_part.shape[0], head_count, HD)
    value_heads = value_part.reshape(value_part.shape[0], head_count, HD)
    allowed = (query_doc[:, None] == key_doc[None, :])[None]
    scores = jnp.einsum("qhd,khd->hqk", query_heads, key_heads, preferred_element_type=jnp.float32)
    prob_rows = jnp.where(allowed, jnp.exp(scores - lse_part[:, :, None]), 0.0)
    grad_value = jnp.einsum(
        "hqk,qhd->khd",
        prob_rows.astype(jnp.bfloat16),
        grad_heads,
        preferred_element_type=jnp.float32,
    )
    grad_probs = jnp.einsum(
        "qhd,khd->hqk", grad_heads, value_heads, preferred_element_type=jnp.float32
    )
    grad_scores = (prob_rows * (grad_probs - delta_part[:, :, None])).astype(jnp.bfloat16)
    grad_query = jnp.einsum(
        "hqk,khd->qhd", grad_scores, key_heads, preferred_element_type=jnp.float32
    )
    grad_key = jnp.einsum(
        "hqk,qhd->khd", grad_scores, query_heads, preferred_element_type=jnp.float32
    )
    return (
        grad_query.reshape(query_part.shape[0], -1),
        grad_key.reshape(key_part.shape[0], -1),
        grad_value.reshape(key_part.shape[0], -1),
    )


def per_device_ring(tokens, doc_lengths, norm_gains, w_qkv, w_out, w_in, w_down, cotangent):
    row_count = tokens.shape[1]
    hidden = tokens[0].astype(jnp.float32)
    lengths = doc_lengths[0]
    group_size = lax.axis_size("ctx")
    my_index = lax.axis_index("ctx")
    doc_here, pos_here = token_layout(lengths, my_index * row_count, row_count)
    gains_full, qkv_full, out_full, in_full, down_full = (
        lax.all_gather(norm_gains, "ctx", axis=1, tiled=True),
        lax.all_gather(w_qkv, "ctx", axis=1, tiled=True),
        lax.all_gather(w_out, "ctx", axis=1, tiled=True),
        lax.all_gather(w_in, "ctx", axis=1, tiled=True),
        lax.all_gather(w_down, "ctx", axis=1, tiled=True),
    )
    gains_float = gains_full.astype(jnp.float32)
    normed_one, inverse_one, scaled_one = layer_norm(hidden, gains_float[0])
    input_one = scaled_one.astype(jnp.bfloat16)
    raw_proj = jnp.einsum("td,cdn->tcn", input_one, qkv_full, preferred_element_type=jnp.float32)
    proj_width = raw_proj.shape[2]
    head_count = proj_width // HD
    scale_value = HD ** (-0.5)
    queries = (rotate(raw_proj[:, 0], pos_here, 1.0) * scale_value).astype(jnp.bfloat16)
    key_rows = rotate(raw_proj[:, 1], pos_here, 1.0).astype(jnp.bfloat16)
    value_rows = raw_proj[:, 2].astype(jnp.bfloat16)
    query_heads = queries.reshape(row_count, head_count, HD)
    top_score = jnp.full((head_count, row_count), masked_score, jnp.float32)
    weighted = jnp.zeros((row_count, proj_width), jnp.float32)
    key_piece = lax.all_gather(key_rows, "ctx", axis=0, tiled=True)
    value_piece = lax.all_gather(value_rows, "ctx", axis=0, tiled=True)
    piece_rows = key_piece.shape[0]
    key_doc, unused_pos = token_layout(lengths, jnp.int32(0), piece_rows)
    allowed = (doc_here[:, None] == key_doc[None, :])[None]
    scores = jnp.einsum(
        "qhd,khd->hqk",
        query_heads,
        key_piece.reshape(piece_rows, head_count, HD),
        preferred_element_type=jnp.float32,
    )
    scores = jnp.where(allowed, scores, masked_score)
    new_top = jnp.maximum(top_score, jnp.max(scores, axis=2))
    weights = jnp.where(allowed, jnp.exp(scores - new_top[:, :, None]), 0.0)
    factor = jnp.exp(top_score - new_top)
    running_sum = jnp.sum(weights, axis=2)
    update = jnp.einsum(
        "hqk,khd->qhd",
        weights.astype(jnp.bfloat16),
        value_piece.reshape(piece_rows, head_count, HD),
        preferred_element_type=jnp.float32,
    )
    weighted = weighted.reshape(row_count, head_count, HD) * factor.T[:, :, None] + update
    top_score, running_sum, weighted = (
        new_top,
        running_sum,
        weighted.reshape(row_count, proj_width),
    )
    log_total = top_score + jnp.log(running_sum)
    attn_float = (weighted.reshape(row_count, head_count, HD) / running_sum.T[:, :, None]).reshape(
        row_count, proj_width
    )
    attn_low = attn_float.astype(jnp.bfloat16)
    partial_out = jnp.dot(attn_low, out_full, preferred_element_type=jnp.float32)
    branch_one = lax.psum(partial_out.astype(jnp.bfloat16), "head").astype(jnp.float32)
    resid_one = hidden + branch_one
    normed_two, inverse_two, scaled_two = layer_norm(resid_one, gains_float[1])
    input_two = scaled_two.astype(jnp.bfloat16)
    gate_up = jnp.einsum("td,cdf->tcf", input_two, in_full, preferred_element_type=jnp.float32)
    activated, gelu_back = jax.vjp(exact_gelu, gate_up[:, 0])
    mixed_low = (activated * gate_up[:, 1]).astype(jnp.bfloat16)
    partial_ffn = jnp.dot(mixed_low, down_full, preferred_element_type=jnp.float32)
    branch_two = lax.psum(partial_ffn.astype(jnp.bfloat16), "head").astype(jnp.float32)
    result = (resid_one + branch_two).astype(jnp.bfloat16)
    gains_back, qkv_back, out_back, in_back, down_back = (
        gains_float,
        qkv_full,
        out_full,
        in_full,
        down_full,
    )
    grad_rows = cotangent[0]
    grad_down = jnp.einsum("tf,td->fd", mixed_low, grad_rows, preferred_element_type=jnp.float32)
    grad_mixed = jnp.einsum("td,fd->tf", grad_rows, down_back, preferred_element_type=jnp.float32)
    grad_gate = gelu_back(grad_mixed * gate_up[:, 1])[0]
    grad_up = grad_mixed * activated
    grad_gate_up = jnp.stack([grad_gate, grad_up], axis=1).astype(jnp.bfloat16)
    grad_in = jnp.einsum("td,tcf->cdf", input_two, grad_gate_up, preferred_element_type=jnp.float32)
    partial_two = jnp.einsum(
        "tcf,cdf->td", grad_gate_up, in_back, preferred_element_type=jnp.float32
    )
    grad_input_two = lax.psum(partial_two.astype(jnp.bfloat16), "head").astype(jnp.float32)
    grad_norm_two, gain_grad_two = norm_back(grad_input_two, normed_two, inverse_two, gains_back[1])
    grad_resid = grad_rows.astype(jnp.float32) + grad_norm_two
    grad_branch = grad_resid.astype(jnp.bfloat16)
    grad_out = jnp.einsum("tn,td->nd", attn_low, grad_branch, preferred_element_type=jnp.float32)
    grad_attn = jnp.einsum(
        "td,nd->tn", grad_branch, out_back, preferred_element_type=jnp.float32
    ).astype(jnp.bfloat16)
    delta_rows = jnp.sum(
        (grad_attn.astype(jnp.float32) * attn_float).reshape(row_count, head_count, HD), axis=2
    ).T
    zero_rows = jnp.zeros((row_count, proj_width), jnp.float32)

    def key_work(step_index, key_block, value_block, key_grad, value_grad, query_grad):
        anchor = (my_index - step_index) % group_size
        key_doc, unused_pos = token_layout(lengths, anchor * row_count, row_count)
        step_grads = back_step(
            queries, grad_attn, log_total, delta_rows, doc_here, key_block, value_block, key_doc
        )
        return (key_grad + step_grads[1], value_grad + step_grads[2], query_grad + step_grads[0])

    def send_key_grads(key_grad, value_grad):
        return (
            passed_along(key_grad.astype(jnp.bfloat16), "ctx", 1).astype(key_grad.dtype),
            passed_along(value_grad.astype(jnp.bfloat16), "ctx", 1).astype(value_grad.dtype),
        )

    def key_turn(step_index, state_now):
        key_block, value_block, key_grad, value_grad, query_grad = state_now
        key_grad, value_grad, query_grad = key_work(
            step_index, key_block, value_block, key_grad, value_grad, query_grad
        )
        key_block, value_block = passed_along((key_block, value_block), "ctx", 1)
        key_grad, value_grad = send_key_grads(key_grad, value_grad)
        return (key_block, value_block, key_grad, value_grad, query_grad)

    state_now = lax.fori_loop(
        0, group_size - 1, key_turn, (key_rows, value_rows, zero_rows, zero_rows, zero_rows)
    )
    last_grads = key_work(
        group_size - 1, state_now[0], state_now[1], state_now[2], state_now[3], state_now[4]
    )
    grad_query = last_grads[2]
    grad_key, grad_value = send_key_grads(last_grads[0], last_grads[1])
    grad_query_pre = rotate(grad_query, pos_here, -1.0) * scale_value
    grad_key_pre = rotate(grad_key, pos_here, -1.0)
    grad_raw = jnp.stack([grad_query_pre, grad_key_pre, grad_value], axis=1).astype(jnp.bfloat16)
    grad_qkv = jnp.einsum("td,tcn->cdn", input_one, grad_raw, preferred_element_type=jnp.float32)
    partial_one = jnp.einsum("tcn,cdn->td", grad_raw, qkv_back, preferred_element_type=jnp.float32)
    grad_input_one = lax.psum(partial_one.astype(jnp.bfloat16), "head").astype(jnp.float32)
    grad_norm_one, gain_grad_one = norm_back(grad_input_one, normed_one, inverse_one, gains_back[0])
    grad_tokens = (grad_resid + grad_norm_one).astype(jnp.bfloat16)
    grad_gains = jnp.stack([gain_grad_one, gain_grad_two])
    share_gains, share_qkv, share_out, share_in, share_down = (
        lax.psum_scatter(
            grad_gains.astype(jnp.bfloat16), "ctx", scatter_dimension=1, tiled=True
        ).astype(jnp.float32),
        lax.psum_scatter(
            grad_qkv.astype(jnp.bfloat16), "ctx", scatter_dimension=1, tiled=True
        ).astype(jnp.float32),
        lax.psum_scatter(
            grad_out.astype(jnp.bfloat16), "ctx", scatter_dimension=1, tiled=True
        ).astype(jnp.float32),
        lax.psum_scatter(
            grad_in.astype(jnp.bfloat16), "ctx", scatter_dimension=1, tiled=True
        ).astype(jnp.float32),
        lax.psum_scatter(
            grad_down.astype(jnp.bfloat16), "ctx", scatter_dimension=1, tiled=True
        ).astype(jnp.float32),
    )
    total_gains, total_qkv, total_out, total_in, total_down = (
        lax.psum(share_gains.astype(jnp.bfloat16), "seq").astype(jnp.float32),
        lax.psum(share_qkv.astype(jnp.bfloat16), "seq").astype(jnp.float32),
        lax.psum(share_out.astype(jnp.bfloat16), "seq").astype(jnp.float32),
        lax.psum(share_in.astype(jnp.bfloat16), "seq").astype(jnp.float32),
        lax.psum(share_down.astype(jnp.bfloat16), "seq").astype(jnp.float32),
    )
    return (
        result[None],
        grad_tokens[None],
        total_gains,
        total_qkv,
        total_out,
        total_in,
        total_down,
    )


def pair_swap(block, axis, mask):
    size = lax.axis_size(axis)
    return lax.ppermute(block, axis, [(i, i ^ mask) for i in range(size)])


def gather_weight(weight, dim):
    group = lax.axis_size("ctx")
    if group > 4:
        return lax.all_gather(weight, "ctx", axis=dim, tiled=True)
    me = lax.axis_index("ctx")
    seq = lax.axis_index("seq")
    half = weight.shape[dim] // 2
    mine = lax.dynamic_slice_in_dim(weight, seq * half, half, dim)
    near = jnp.stack([passed_along(mine, "ctx", k) for k in range(1, group)])
    far = pair_swap(near, "seq", 1)
    first = seq == 0
    whole = jnp.concatenate(
        [jnp.where(first, near, far), jnp.where(first, far, near)], axis=dim + 1
    )
    pieces = [weight] + [whole[k] for k in range(group - 1)]
    stacked = jnp.stack(pieces)
    ordered = [
        lax.dynamic_index_in_dim(stacked, (me - j) % group, 0, keepdims=False)
        for j in range(group)
    ]
    return jnp.concatenate(ordered, axis=dim)


def gather_gains(gains):
    group = lax.axis_size("ctx")
    if group > 4:
        return lax.all_gather(gains, "ctx", axis=1, tiled=True)
    me = lax.axis_index("ctx")
    width = gains.shape[1]
    full = jnp.zeros((gains.shape[0], width * group), gains.dtype)
    for k in range(group):
        block = gains if k == 0 else passed_along(gains, "ctx", k)
        full = lax.dynamic_update_slice_in_dim(full, block, ((me - k) % group) * width, 1)
    return full


def reduce_weight(grad):
    group = lax.axis_size("ctx")
    me = lax.axis_index("ctx")
    seq = lax.axis_index("seq")
    a, rows, b = grad.shape
    half = rows // group // 2
    split = grad.reshape(a, group, 2, half, b)
    keep = lax.dynamic_index_in_dim(split, seq, 2, keepdims=False)
    give = lax.dynamic_index_in_dim(split, 1 - seq, 2, keepdims=False).astype(jnp.bfloat16)
    both = keep + pair_swap(give, "seq", 1).astype(jnp.float32)
    share = lax.dynamic_index_in_dim(both, me, 1, keepdims=False)
    low_both = both.astype(jnp.bfloat16)
    for k in range(1, group):
        block = lax.dynamic_index_in_dim(low_both, (me + k) % group, 1, keepdims=False)
        share = share + passed_along(block, "ctx", k).astype(jnp.float32)
    return share.astype(jnp.bfloat16)


def reduce_weight_rows(share):
    other = pair_swap(share, "seq", 1)
    first = lax.axis_index("seq") == 0
    low_part = jnp.where(first, share, other)
    high_part = jnp.where(first, other, share)
    return jnp.concatenate([low_part, high_part], axis=1).astype(jnp.float32)


def reduce_gains(grads):
    group = lax.axis_size("ctx")
    me = lax.axis_index("ctx")
    width = grads.shape[1] // group
    if group > 4:
        share = lax.psum_scatter(grads, "ctx", scatter_dimension=1, tiled=True)
    else:
        share = lax.dynamic_slice_in_dim(grads, me * width, width, 1)
        for k in range(1, group):
            block = lax.dynamic_slice_in_dim(grads, ((me + k) % group) * width, width, 1)
            share = share + passed_along(block, "ctx", k)
    return share + pair_swap(share, "seq", 1)


def head_sum(partial):
    half = partial.shape[0] // 2
    core = lax.axis_index("head") % 2
    mine = lax.dynamic_slice_in_dim(partial, core * half, half, 0)
    theirs = lax.dynamic_slice_in_dim(partial, (1 - core) * half, half, 0).astype(jnp.bfloat16)
    pair = (mine + pair_swap(theirs, "head", 1).astype(jnp.float32)).astype(jnp.bfloat16)
    far = pair_swap(pair, "head", 2)
    total = (pair.astype(jnp.float32) + far.astype(jnp.float32)).astype(jnp.bfloat16)
    other = pair_swap(total, "head", 1)
    first = core == 0
    return jnp.concatenate(
        [jnp.where(first, total, other), jnp.where(first, other, total)], axis=0
    ).astype(jnp.float32)


def swap_blocks(blocks, sign):
    group = lax.axis_size("ctx")
    me = lax.axis_index("ctx")
    got = [lax.dynamic_index_in_dim(blocks, me, 0, keepdims=False)]
    for k in range(1, group):
        send = lax.dynamic_index_in_dim(blocks, (me + k) % group, 0, keepdims=False)
        got.append(passed_along(send, "ctx", k))
    stacked = jnp.stack(got)
    return [
        lax.dynamic_index_in_dim(stacked, (me - j) % group, 0, keepdims=False)
        for j in range(group)
    ]


def turn(values, cosine, sine):
    half = HD // 2
    lower, upper = values[..., :half, :], values[..., half:, :]
    return jnp.concatenate(
        [lower * cosine - upper * sine, upper * cosine + lower * sine], axis=-2
    )


def tables(positions):
    frequency = theta_base ** (-(jnp.arange(HD // 2, dtype=jnp.float32) * (2.0 / HD)))
    angles = frequency[:, None] * positions.astype(jnp.float32)[None, :]
    return (jnp.cos(angles), jnp.sin(angles))


def attend_kernel(tile, span_ref, q_ref, k_ref, v_ref, row_doc_ref, col_doc_ref, out_ref, lse_ref, keys_scr):
    step = pl.program_id(0)

    @pl.when(step == 0)
    def _():
        keys_scr[...] = k_ref[...].T

    q = q_ref[...]
    doc = row_doc_ref[...]
    first, last = span_ref[0, step], span_ref[1, step]

    def body(j, state):
        top, total, out = state
        at = pl.multiple_of(j * tile, tile)
        s = jnp.dot(keys_scr[pl.ds(at, tile), :], q, preferred_element_type=jnp.float32)
        allowed = col_doc_ref[pl.ds(at, tile), :] == doc
        s = jnp.where(allowed, s, masked_score)
        new_top = jnp.maximum(top, jnp.max(s, axis=0, keepdims=True))
        e = jnp.where(allowed, jnp.exp(s - new_top), 0.0)
        factor = jnp.exp(top - new_top)
        total = total * factor + jnp.sum(e, axis=0, keepdims=True)
        out = out * factor + jnp.dot(
            v_ref[:, pl.ds(at, tile)], e.astype(jnp.bfloat16), preferred_element_type=jnp.float32
        )
        return (new_top, total, out)

    width = q.shape[1]
    state = (
        jnp.full((1, width), masked_score, jnp.float32),
        jnp.zeros((1, width), jnp.float32),
        jnp.zeros((HD, width), jnp.float32),
    )
    top, total, out = lax.fori_loop(first, last, body, state)
    out_ref[...] = out / total
    lse_ref[...] = top + jnp.log(total)


def attend_back_kernel(
    tile, span_ref, q_ref, k_ref, v_ref, row_doc_ref, col_doc_ref, lse_ref, out_ref, grad_ref,
    dq_ref, dk_ref, dv_ref, keys_scr, values_scr,
):
    step = pl.program_id(0)

    @pl.when(step == 0)
    def _():
        keys_scr[...] = k_ref[...].T
        values_scr[...] = v_ref[...].T
        dk_ref[...] = jnp.zeros_like(dk_ref)
        dv_ref[...] = jnp.zeros_like(dv_ref)

    q = q_ref[...]
    grad = grad_ref[...]
    delta = jnp.sum(grad.astype(jnp.float32) * out_ref[...], axis=0, keepdims=True)
    doc = row_doc_ref[...]
    lse = lse_ref[...]
    q_rows = q.T
    grad_rows = grad.T
    first, last = span_ref[0, step], span_ref[1, step]

    def body(j, dq):
        at = pl.multiple_of(j * tile, tile)
        s = jnp.dot(keys_scr[pl.ds(at, tile), :], q, preferred_element_type=jnp.float32)
        allowed = col_doc_ref[pl.ds(at, tile), :] == doc
        p = jnp.where(allowed, jnp.exp(s - lse), 0.0)
        dp = jnp.dot(values_scr[pl.ds(at, tile), :], grad, preferred_element_type=jnp.float32)
        ds = (p * (dp - delta)).astype(jnp.bfloat16)
        dv_ref[pl.ds(at, tile), :] += jnp.dot(
            p.astype(jnp.bfloat16), grad_rows, preferred_element_type=jnp.float32
        )
        dk_ref[pl.ds(at, tile), :] += jnp.dot(ds, q_rows, preferred_element_type=jnp.float32)
        return dq + jnp.dot(
            k_ref[:, pl.ds(at, tile)], ds, preferred_element_type=jnp.float32
        )

    dq_ref[...] = lax.fori_loop(first, last, body, jnp.zeros(q.shape, jnp.float32))


def tile_spans(lengths, tiles, tile):
    ends = jnp.cumsum(lengths, dtype=jnp.int32)
    starts = ends - lengths
    low_row = jnp.arange(tiles, dtype=jnp.int32) * tile
    high_row = low_row + (tile - 1)
    low_doc = jnp.sum((low_row[:, None] >= ends[None, :]).astype(jnp.int32), axis=1)
    high_doc = jnp.sum((high_row[:, None] >= ends[None, :]).astype(jnp.int32), axis=1)
    slots = jnp.arange(lengths.shape[0], dtype=jnp.int32)[None, :]
    begin = jnp.sum(jnp.where(slots == low_doc[:, None], starts[None, :], 0), axis=1)
    finish = jnp.sum(jnp.where(slots == high_doc[:, None], ends[None, :], 0), axis=1)
    return jnp.stack([begin // tile, (finish + (tile - 1)) // tile]).astype(jnp.int32)


def head_specs(tile, total):
    moving = pl.BlockSpec((HD, tile), lambda i, span: (0, i))
    whole = pl.BlockSpec((HD, total), lambda i, span: (0, 0))
    row = pl.BlockSpec((1, tile), lambda i, span: (0, i))
    column = pl.BlockSpec((total, 1), lambda i, span: (0, 0))
    return (moving, whole, row, column)


def attend(q, k, v, doc, spans, tile):
    total = q.shape[1]
    moving, whole, row, column = head_specs(tile, total)
    return pl.pallas_call(
        functools.partial(attend_kernel, tile),
        grid_spec=pltpu.PrefetchScalarGridSpec(
            num_scalar_prefetch=1,
            grid=(total // tile,),
            in_specs=[moving, whole, whole, row, column],
            out_specs=[moving, row],
            scratch_shapes=[pltpu.VMEM((total, HD), jnp.bfloat16)],
        ),
        out_shape=[
            jax.ShapeDtypeStruct((HD, total), jnp.float32),
            jax.ShapeDtypeStruct((1, total), jnp.float32),
        ],
        compiler_params=pltpu.CompilerParams(vmem_limit_bytes=40 * 1024 * 1024),
        cost_estimate=pl.CostEstimate(
            flops=10 * total * total * HD, bytes_accessed=4 * total * HD, transcendentals=total * total
        ),
        name="attend",
    )(spans, q, k, v, doc[None, :], doc[:, None])


def attend_back(q, k, v, doc, spans, tile, lse, out, grad):
    total = q.shape[1]
    moving, whole, row, column = head_specs(tile, total)
    tall = pl.BlockSpec((total, HD), lambda i, span: (0, 0))
    dq, dk, dv = pl.pallas_call(
        functools.partial(attend_back_kernel, tile),
        grid_spec=pltpu.PrefetchScalarGridSpec(
            num_scalar_prefetch=1,
            grid=(total // tile,),
            in_specs=[moving, whole, whole, row, column, row, moving, moving],
            out_specs=[moving, tall, tall],
            scratch_shapes=[
                pltpu.VMEM((total, HD), jnp.bfloat16),
                pltpu.VMEM((total, HD), jnp.bfloat16),
            ],
        ),
        out_shape=[
            jax.ShapeDtypeStruct((HD, total), jnp.float32),
            jax.ShapeDtypeStruct((total, HD), jnp.float32),
            jax.ShapeDtypeStruct((total, HD), jnp.float32),
        ],
        compiler_params=pltpu.CompilerParams(vmem_limit_bytes=40 * 1024 * 1024),
        cost_estimate=pl.CostEstimate(
            flops=20 * total * total * HD, bytes_accessed=4 * total * HD, transcendentals=total * total
        ),
        name="attend_back",
    )(spans, q, k, v, doc[None, :], doc[:, None], lse, out, grad)
    return (dq, dk.T, dv.T)


def per_device(tokens, doc_lengths, norm_gains, w_qkv, w_out, w_in, w_down, cotangent):
    rows = tokens.shape[1]
    hidden = tokens[0].astype(jnp.float32)
    lengths = doc_lengths[0]
    group = lax.axis_size("ctx")
    me = lax.axis_index("ctx")
    width = w_qkv.shape[2]
    heads = width // HD
    each = heads // group
    scale = HD ** (-0.5)
    gains = gather_gains(norm_gains).astype(jnp.float32)
    qkv_full = gather_weight(w_qkv, 1)
    tail_full = gather_weight(jnp.concatenate([w_out, w_down], axis=0), 1)
    out_full, down_full = (tail_full[:width], tail_full[width:])
    in_full = gather_weight(w_in, 1)
    doc_all, pos_all = token_layout(lengths, jnp.int32(0), rows * group)
    cos_all, sin_all = tables(pos_all)
    cos_here = lax.dynamic_slice_in_dim(cos_all, me * rows, rows, 1)
    sin_here = lax.dynamic_slice_in_dim(sin_all, me * rows, rows, 1)

    normed_one, inverse_one, scaled_one = layer_norm(hidden, gains[0])
    input_one = scaled_one.astype(jnp.bfloat16)
    raw = jnp.einsum("cdn,td->cnt", qkv_full, input_one, preferred_element_type=jnp.float32)
    raw = raw.reshape(3, heads, HD, rows)
    q = (turn(raw[0], cos_here, sin_here) * scale).astype(jnp.bfloat16)
    k = turn(raw[1], cos_here, sin_here).astype(jnp.bfloat16)
    v = raw[2].astype(jnp.bfloat16)
    blocks = jnp.stack([q, k, v], axis=1).reshape(group, each, 3, HD, rows)
    mine = jnp.concatenate(swap_blocks(blocks, 1), axis=-1)
    q, k, v = (mine[:, 0], mine[:, 1], mine[:, 2])
    q, k, v = (q.reshape(HD, -1), k.reshape(HD, -1), v.reshape(HD, -1))
    tile = 512 if rows * group % 512 == 0 else 128
    spans = tile_spans(lengths, rows * group // tile, tile)
    attn_float, lse = attend(q, k, v, doc_all, spans, tile)
    parts = attn_float.astype(jnp.bfloat16).reshape(each, HD, group, rows).transpose(2, 0, 1, 3)
    attn_low = jnp.concatenate(swap_blocks(parts, -1), axis=0).reshape(width, rows)

    partial_out = jnp.einsum("nt,nd->td", attn_low, out_full, preferred_element_type=jnp.float32)
    resid_one = hidden + head_sum(partial_out)
    normed_two, inverse_two, scaled_two = layer_norm(resid_one, gains[1])
    input_two = scaled_two.astype(jnp.bfloat16)
    gate_up = jnp.einsum("td,cdf->tcf", input_two, in_full, preferred_element_type=jnp.float32)
    activated, gelu_back = jax.vjp(exact_gelu, gate_up[:, 0])
    mixed_low = (activated * gate_up[:, 1]).astype(jnp.bfloat16)
    partial_ffn = jnp.dot(mixed_low, down_full, preferred_element_type=jnp.float32)

    grad_rows = cotangent[0]
    grad_mixed = jnp.einsum("td,fd->tf", grad_rows, down_full, preferred_element_type=jnp.float32)
    grad_gate = gelu_back(grad_mixed * gate_up[:, 1])[0]
    grad_up = grad_mixed * activated
    grad_gate_up = jnp.stack([grad_gate, grad_up], axis=1).astype(jnp.bfloat16)
    partial_two = jnp.einsum(
        "tcf,cdf->td", grad_gate_up, in_full, preferred_element_type=jnp.float32
    )
    grad_input_two = head_sum(partial_two)
    grad_down = jnp.einsum(
        "tf,td->df", mixed_low, grad_rows, preferred_element_type=jnp.float32
    )
    grad_in = jnp.einsum(
        "td,tcf->cdf", input_two, grad_gate_up, preferred_element_type=jnp.float32
    )
    grad_input_two, grad_down, grad_in = lax.optimization_barrier(
        (grad_input_two, grad_down, grad_in)
    )
    share_down = reduce_weight(grad_down[None])
    share_in = reduce_weight(grad_in)
    result = (resid_one + head_sum(partial_ffn)).astype(jnp.bfloat16)
    grad_norm_two, gain_grad_two = norm_back(grad_input_two, normed_two, inverse_two, gains[1])
    grad_resid = grad_rows.astype(jnp.float32) + grad_norm_two
    grad_branch = grad_resid.astype(jnp.bfloat16)
    grad_attn = jnp.einsum(
        "nd,td->nt", out_full, grad_branch, preferred_element_type=jnp.float32
    ).astype(jnp.bfloat16)
    grad_mine = jnp.concatenate(
        swap_blocks(grad_attn.reshape(group, each, HD, rows), 1), axis=-1
    )
    grad_out = jnp.einsum(
        "nt,td->dn", attn_low, grad_branch, preferred_element_type=jnp.float32
    )
    grad_mine, grad_out = lax.optimization_barrier((grad_mine, grad_out))
    share_out = reduce_weight(grad_out[None])
    grad_q, grad_k, grad_v = attend_back(
        q, k, v, doc_all, spans, tile, lse, attn_float, grad_mine.reshape(HD, -1)
    )
    grad_q = turn(grad_q, cos_all, -sin_all) * scale
    grad_k = turn(grad_k, cos_all, -sin_all)
    back = jnp.stack([grad_q, grad_k, grad_v]).astype(jnp.bfloat16)
    back = back.reshape(each, 3, HD, group, rows).transpose(3, 0, 1, 2, 4)
    grad_raw = jnp.concatenate(swap_blocks(back, -1), axis=0)
    grad_raw = grad_raw.transpose(1, 0, 2, 3).reshape(3, width, rows)
    partial_one = jnp.einsum(
        "cnt,cdn->td", grad_raw, qkv_full, preferred_element_type=jnp.float32
    )
    grad_qkv = jnp.einsum(
        "td,cnt->cdn", input_one, grad_raw, preferred_element_type=jnp.float32
    )
    share_qkv = reduce_weight(grad_qkv)
    grad_input_one = head_sum(partial_one)
    grad_norm_one, gain_grad_one = norm_back(grad_input_one, normed_one, inverse_one, gains[0])
    grad_tokens = (grad_resid + grad_norm_one).astype(jnp.bfloat16)
    total_gains = reduce_gains(jnp.stack([gain_grad_one, gain_grad_two]))
    return (
        result[None],
        grad_tokens[None],
        total_gains,
        reduce_weight_rows(share_qkv),
        reduce_weight_rows(share_out)[0].T,
        reduce_weight_rows(share_in),
        reduce_weight_rows(share_down)[0].T,
    )


def solution(mesh):
    heads = 1024 // HD // mesh.shape["head"]
    body = per_device if heads == mesh.shape["ctx"] else per_device_ring
    return jax.shard_map(
        body,
        mesh=mesh,
        in_specs=(
            P("seq", "ctx", None),
            P("seq", None),
            P(None, "ctx"),
            P(None, "ctx", "head"),
            P("head", "ctx"),
            P(None, "ctx", "head"),
            P("head", "ctx"),
            P("seq", "ctx", None),
        ),
        out_specs=(
            P("seq", "ctx", None),
            P("seq", "ctx", None),
            P(None, "ctx"),
            P(None, "ctx", "head"),
            P("head", "ctx"),
            P(None, "ctx", "head"),
            P("head", "ctx"),
        ),
        check_vma=False,
    )
```

```python
import functools
import jax
import jax.numpy as jnp
from jax import lax
from jax.experimental import pallas as pl
from jax.experimental.pallas import tpu as pltpu
from jax.sharding import PartitionSpec as P

HD = 64


norm_eps = 1e-05
theta_base = 160000.0
masked_score = -1e30


def passed_along(block, axis, distance):
    devices = range(lax.axis_size(axis))
    route = [((i - distance) % len(devices), i) for i in devices]
    return lax.ppermute(block, axis, route)


def token_layout(lengths, first_row, row_count):
    doc_ends = jnp.cumsum(lengths, dtype=jnp.int32)
    places = first_row + jnp.arange(row_count, dtype=jnp.int32)
    passed = places[:, None] >= doc_ends[None, :]
    doc_index = jnp.sum(passed.astype(jnp.int32), axis=1, dtype=jnp.int32)
    starts = jnp.sum(jnp.where(passed, lengths[None, :], 0), axis=1, dtype=jnp.int32)
    return (doc_index, places - starts)


def rotate(values, positions, turn_sign):
    leading = values.shape[:-1]
    head_count = values.shape[-1] // HD
    half_width = HD // 2
    frequency = theta_base ** (-(jnp.arange(half_width, dtype=jnp.float32) * (2.0 / HD)))
    angles = positions.astype(jnp.float32)[..., None] * frequency
    cosine = jnp.cos(angles)[..., None, :]
    sine_part = turn_sign * jnp.sin(angles)[..., None, :]
    shaped = values.reshape(leading + (head_count, HD))
    lower_half = shaped[..., :half_width]
    upper_half = shaped[..., half_width:]
    turned = jnp.concatenate(
        [
            lower_half * cosine - upper_half * sine_part,
            upper_half * cosine + lower_half * sine_part,
        ],
        axis=-1,
    )
    return turned.reshape(values.shape)


def layer_norm(values, gain_row):
    mean_value = jnp.mean(values, axis=-1, keepdims=True)
    centered = values - mean_value
    variance = jnp.mean(centered * centered, axis=-1, keepdims=True)
    inverse = lax.rsqrt(variance + norm_eps)
    normed = centered * inverse
    return (normed, inverse, normed * gain_row)


def norm_back(grad_scaled, normed, inverse, gain_row):
    grad_normed = grad_scaled * gain_row
    mean_grad = jnp.mean(grad_normed, axis=-1, keepdims=True)
    mean_proj = jnp.mean(grad_normed * normed, axis=-1, keepdims=True)
    grad_values = inverse * (grad_normed - mean_grad - normed * mean_proj)
    return (grad_values, jnp.sum(grad_scaled * normed, axis=0))


def exact_gelu(values):
    return jax.nn.gelu(values, approximate=False)


def back_step(
    query_part, grad_part, lse_part, delta_part, query_doc, key_part, value_part, key_doc
):
    head_count = query_part.shape[1] // HD
    query_heads = query_part.reshape(query_part.shape[0], head_count, HD)
    grad_heads = grad_part.reshape(grad_part.shape[0], head_count, HD)
    key_heads = key_part.reshape(key_part.shape[0], head_count, HD)
    value_heads = value_part.reshape(value_part.shape[0], head_count, HD)
    allowed = (query_doc[:, None] == key_doc[None, :])[None]
    scores = jnp.einsum("qhd,khd->hqk", query_heads, key_heads, preferred_element_type=jnp.float32)
    prob_rows = jnp.where(allowed, jnp.exp(scores - lse_part[:, :, None]), 0.0)
    grad_value = jnp.einsum(
        "hqk,qhd->khd",
        prob_rows.astype(jnp.bfloat16),
        grad_heads,
        preferred_element_type=jnp.float32,
    )
    grad_probs = jnp.einsum(
        "qhd,khd->hqk", grad_heads, value_heads, preferred_element_type=jnp.float32
    )
    grad_scores = (prob_rows * (grad_probs - delta_part[:, :, None])).astype(jnp.bfloat16)
    grad_query = jnp.einsum(
        "hqk,khd->qhd", grad_scores, key_heads, preferred_element_type=jnp.float32
    )
    grad_key = jnp.einsum(
        "hqk,qhd->khd", grad_scores, query_heads, preferred_element_type=jnp.float32
    )
    return (
        grad_query.reshape(query_part.shape[0], -1),
        grad_key.reshape(key_part.shape[0], -1),
        grad_value.reshape(key_part.shape[0], -1),
    )


def per_device_ring(tokens, doc_lengths, norm_gains, w_qkv, w_out, w_in, w_down, cotangent):
    row_count = tokens.shape[1]
    hidden = tokens[0].astype(jnp.float32)
    lengths = doc_lengths[0]
    group_size = lax.axis_size("ctx")
    my_index = lax.axis_index("ctx")
    doc_here, pos_here = token_layout(lengths, my_index * row_count, row_count)
    gains_full, qkv_full, out_full, in_full, down_full = (
        lax.all_gather(norm_gains, "ctx", axis=1, tiled=True),
        lax.all_gather(w_qkv, "ctx", axis=1, tiled=True),
        lax.all_gather(w_out, "ctx", axis=1, tiled=True),
        lax.all_gather(w_in, "ctx", axis=1, tiled=True),
        lax.all_gather(w_down, "ctx", axis=1, tiled=True),
    )
    gains_float = gains_full.astype(jnp.float32)
    normed_one, inverse_one, scaled_one = layer_norm(hidden, gains_float[0])
    input_one = scaled_one.astype(jnp.bfloat16)
    raw_proj = jnp.einsum("td,cdn->tcn", input_one, qkv_full, preferred_element_type=jnp.float32)
    proj_width = raw_proj.shape[2]
    head_count = proj_width // HD
    scale_value = HD ** (-0.5)
    queries = (rotate(raw_proj[:, 0], pos_here, 1.0) * scale_value).astype(jnp.bfloat16)
    key_rows = rotate(raw_proj[:, 1], pos_here, 1.0).astype(jnp.bfloat16)
    value_rows = raw_proj[:, 2].astype(jnp.bfloat16)
    query_heads = queries.reshape(row_count, head_count, HD)
    top_score = jnp.full((head_count, row_count), masked_score, jnp.float32)
    weighted = jnp.zeros((row_count, proj_width), jnp.float32)
    key_piece = lax.all_gather(key_rows, "ctx", axis=0, tiled=True)
    value_piece = lax.all_gather(value_rows, "ctx", axis=0, tiled=True)
    piece_rows = key_piece.shape[0]
    key_doc, unused_pos = token_layout(lengths, jnp.int32(0), piece_rows)
    allowed = (doc_here[:, None] == key_doc[None, :])[None]
    scores = jnp.einsum(
        "qhd,khd->hqk",
        query_heads,
        key_piece.reshape(piece_rows, head_count, HD),
        preferred_element_type=jnp.float32,
    )
    scores = jnp.where(allowed, scores, masked_score)
    new_top = jnp.maximum(top_score, jnp.max(scores, axis=2))
    weights = jnp.where(allowed, jnp.exp(scores - new_top[:, :, None]), 0.0)
    factor = jnp.exp(top_score - new_top)
    running_sum = jnp.sum(weights, axis=2)
    update = jnp.einsum(
        "hqk,khd->qhd",
        weights.astype(jnp.bfloat16),
        value_piece.reshape(piece_rows, head_count, HD),
        preferred_element_type=jnp.float32,
    )
    weighted = weighted.reshape(row_count, head_count, HD) * factor.T[:, :, None] + update
    top_score, running_sum, weighted = (
        new_top,
        running_sum,
        weighted.reshape(row_count, proj_width),
    )
    log_total = top_score + jnp.log(running_sum)
    attn_float = (weighted.reshape(row_count, head_count, HD) / running_sum.T[:, :, None]).reshape(
        row_count, proj_width
    )
    attn_low = attn_float.astype(jnp.bfloat16)
    partial_out = jnp.dot(attn_low, out_full, preferred_element_type=jnp.float32)
    branch_one = lax.psum(partial_out.astype(jnp.bfloat16), "head").astype(jnp.float32)
    resid_one = hidden + branch_one
    normed_two, inverse_two, scaled_two = layer_norm(resid_one, gains_float[1])
    input_two = scaled_two.astype(jnp.bfloat16)
    gate_up = jnp.einsum("td,cdf->tcf", input_two, in_full, preferred_element_type=jnp.float32)
    activated, gelu_back = jax.vjp(exact_gelu, gate_up[:, 0])
    mixed_low = (activated * gate_up[:, 1]).astype(jnp.bfloat16)
    partial_ffn = jnp.dot(mixed_low, down_full, preferred_element_type=jnp.float32)
    branch_two = lax.psum(partial_ffn.astype(jnp.bfloat16), "head").astype(jnp.float32)
    result = (resid_one + branch_two).astype(jnp.bfloat16)
    gains_back, qkv_back, out_back, in_back, down_back = (
        gains_float,
        qkv_full,
        out_full,
        in_full,
        down_full,
    )
    grad_rows = cotangent[0]
    grad_down = jnp.einsum("tf,td->fd", mixed_low, grad_rows, preferred_element_type=jnp.float32)
    grad_mixed = jnp.einsum("td,fd->tf", grad_rows, down_back, preferred_element_type=jnp.float32)
    grad_gate = gelu_back(grad_mixed * gate_up[:, 1])[0]
    grad_up = grad_mixed * activated
    grad_gate_up = jnp.stack([grad_gate, grad_up], axis=1).astype(jnp.bfloat16)
    grad_in = jnp.einsum("td,tcf->cdf", input_two, grad_gate_up, preferred_element_type=jnp.float32)
    partial_two = jnp.einsum(
        "tcf,cdf->td", grad_gate_up, in_back, preferred_element_type=jnp.float32
    )
    grad_input_two = lax.psum(partial_two.astype(jnp.bfloat16), "head").astype(jnp.float32)
    grad_norm_two, gain_grad_two = norm_back(grad_input_two, normed_two, inverse_two, gains_back[1])
    grad_resid = grad_rows.astype(jnp.float32) + grad_norm_two
    grad_branch = grad_resid.astype(jnp.bfloat16)
    grad_out = jnp.einsum("tn,td->nd", attn_low, grad_branch, preferred_element_type=jnp.float32)
    grad_attn = jnp.einsum(
        "td,nd->tn", grad_branch, out_back, preferred_element_type=jnp.float32
    ).astype(jnp.bfloat16)
    delta_rows = jnp.sum(
        (grad_attn.astype(jnp.float32) * attn_float).reshape(row_count, head_count, HD), axis=2
    ).T
    zero_rows = jnp.zeros((row_count, proj_width), jnp.float32)

    def key_work(step_index, key_block, value_block, key_grad, value_grad, query_grad):
        anchor = (my_index - step_index) % group_size
        key_doc, unused_pos = token_layout(lengths, anchor * row_count, row_count)
        step_grads = back_step(
            queries, grad_attn, log_total, delta_rows, doc_here, key_block, value_block, key_doc
        )
        return (key_grad + step_grads[1], value_grad + step_grads[2], query_grad + step_grads[0])

    def send_key_grads(key_grad, value_grad):
        return (
            passed_along(key_grad.astype(jnp.bfloat16), "ctx", 1).astype(key_grad.dtype),
            passed_along(value_grad.astype(jnp.bfloat16), "ctx", 1).astype(value_grad.dtype),
        )

    def key_turn(step_index, state_now):
        key_block, value_block, key_grad, value_grad, query_grad = state_now
        key_grad, value_grad, query_grad = key_work(
            step_index, key_block, value_block, key_grad, value_grad, query_grad
        )
        key_block, value_block = passed_along((key_block, value_block), "ctx", 1)
        key_grad, value_grad = send_key_grads(key_grad, value_grad)
        return (key_block, value_block, key_grad, value_grad, query_grad)

    state_now = lax.fori_loop(
        0, group_size - 1, key_turn, (key_rows, value_rows, zero_rows, zero_rows, zero_rows)
    )
    last_grads = key_work(
        group_size - 1, state_now[0], state_now[1], state_now[2], state_now[3], state_now[4]
    )
    grad_query = last_grads[2]
    grad_key, grad_value = send_key_grads(last_grads[0], last_grads[1])
    grad_query_pre = rotate(grad_query, pos_here, -1.0) * scale_value
    grad_key_pre = rotate(grad_key, pos_here, -1.0)
    grad_raw = jnp.stack([grad_query_pre, grad_key_pre, grad_value], axis=1).astype(jnp.bfloat16)
    grad_qkv = jnp.einsum("td,tcn->cdn", input_one, grad_raw, preferred_element_type=jnp.float32)
    partial_one = jnp.einsum("tcn,cdn->td", grad_raw, qkv_back, preferred_element_type=jnp.float32)
    grad_input_one = lax.psum(partial_one.astype(jnp.bfloat16), "head").astype(jnp.float32)
    grad_norm_one, gain_grad_one = norm_back(grad_input_one, normed_one, inverse_one, gains_back[0])
    grad_tokens = (grad_resid + grad_norm_one).astype(jnp.bfloat16)
    grad_gains = jnp.stack([gain_grad_one, gain_grad_two])
    share_gains, share_qkv, share_out, share_in, share_down = (
        lax.psum_scatter(
            grad_gains.astype(jnp.bfloat16), "ctx", scatter_dimension=1, tiled=True
        ).astype(jnp.float32),
        lax.psum_scatter(
            grad_qkv.astype(jnp.bfloat16), "ctx", scatter_dimension=1, tiled=True
        ).astype(jnp.float32),
        lax.psum_scatter(
            grad_out.astype(jnp.bfloat16), "ctx", scatter_dimension=1, tiled=True
        ).astype(jnp.float32),
        lax.psum_scatter(
            grad_in.astype(jnp.bfloat16), "ctx", scatter_dimension=1, tiled=True
        ).astype(jnp.float32),
        lax.psum_scatter(
            grad_down.astype(jnp.bfloat16), "ctx", scatter_dimension=1, tiled=True
        ).astype(jnp.float32),
    )
    total_gains, total_qkv, total_out, total_in, total_down = (
        lax.psum(share_gains.astype(jnp.bfloat16), "seq").astype(jnp.float32),
        lax.psum(share_qkv.astype(jnp.bfloat16), "seq").astype(jnp.float32),
        lax.psum(share_out.astype(jnp.bfloat16), "seq").astype(jnp.float32),
        lax.psum(share_in.astype(jnp.bfloat16), "seq").astype(jnp.float32),
        lax.psum(share_down.astype(jnp.bfloat16), "seq").astype(jnp.float32),
    )
    return (
        result[None],
        grad_tokens[None],
        total_gains,
        total_qkv,
        total_out,
        total_in,
        total_down,
    )


def pair_swap(block, axis, mask):
    size = lax.axis_size(axis)
    return lax.ppermute(block, axis, [(i, i ^ mask) for i in range(size)])


def gather_weight(weight, dim):
    group = lax.axis_size("ctx")
    if group > 4:
        return lax.all_gather(weight, "ctx", axis=dim, tiled=True)
    me = lax.axis_index("ctx")
    seq = lax.axis_index("seq")
    half = weight.shape[dim] // 2
    mine = lax.dynamic_slice_in_dim(weight, seq * half, half, dim)
    near = jnp.stack([passed_along(mine, "ctx", k) for k in range(1, group)])
    far = pair_swap(near, "seq", 1)
    first = seq == 0
    whole = jnp.concatenate(
        [jnp.where(first, near, far), jnp.where(first, far, near)], axis=dim + 1
    )
    pieces = [weight] + [whole[k] for k in range(group - 1)]
    stacked = jnp.stack(pieces)
    ordered = [
        lax.dynamic_index_in_dim(stacked, (me - j) % group, 0, keepdims=False)
        for j in range(group)
    ]
    return jnp.concatenate(ordered, axis=dim)


def gather_gains(gains):
    group = lax.axis_size("ctx")
    if group > 4:
        return lax.all_gather(gains, "ctx", axis=1, tiled=True)
    me = lax.axis_index("ctx")
    width = gains.shape[1]
    full = jnp.zeros((gains.shape[0], width * group), gains.dtype)
    for k in range(group):
        block = gains if k == 0 else passed_along(gains, "ctx", k)
        full = lax.dynamic_update_slice_in_dim(full, block, ((me - k) % group) * width, 1)
    return full


def reduce_weight(grad):
    group = lax.axis_size("ctx")
    me = lax.axis_index("ctx")
    seq = lax.axis_index("seq")
    grad = grad.astype(jnp.bfloat16)
    a, rows, b = grad.shape
    half = rows // group // 2
    split = grad.reshape(a, group, 2, half, b)
    keep = lax.dynamic_index_in_dim(split, seq, 2, keepdims=False)
    give = lax.dynamic_index_in_dim(split, 1 - seq, 2, keepdims=False).astype(jnp.bfloat16)
    both = keep.astype(jnp.float32) + pair_swap(give, "seq", 1).astype(jnp.float32)
    share = lax.dynamic_index_in_dim(both, me, 1, keepdims=False)
    low_both = both.astype(jnp.bfloat16)
    for k in range(1, group):
        block = lax.dynamic_index_in_dim(low_both, (me + k) % group, 1, keepdims=False)
        share = share + passed_along(block, "ctx", k).astype(jnp.float32)
    return share.astype(jnp.bfloat16)


def reduce_weight_rows(share):
    other = pair_swap(share, "seq", 1)
    first = lax.axis_index("seq") == 0
    low_part = jnp.where(first, share, other)
    high_part = jnp.where(first, other, share)
    return jnp.concatenate([low_part, high_part], axis=1).astype(jnp.float32)


def reduce_gains(grads):
    group = lax.axis_size("ctx")
    me = lax.axis_index("ctx")
    width = grads.shape[1] // group
    if group > 4:
        share = lax.psum_scatter(grads, "ctx", scatter_dimension=1, tiled=True)
    else:
        share = lax.dynamic_slice_in_dim(grads, me * width, width, 1)
        for k in range(1, group):
            block = lax.dynamic_slice_in_dim(grads, ((me + k) % group) * width, width, 1)
            share = share + passed_along(block, "ctx", k)
    return share + pair_swap(share, "seq", 1)


def head_sum(partial):
    half = partial.shape[0] // 2
    core = lax.axis_index("head") % 2
    mine = lax.dynamic_slice_in_dim(partial, core * half, half, 0)
    theirs = lax.dynamic_slice_in_dim(partial, (1 - core) * half, half, 0).astype(jnp.bfloat16)
    pair = (mine + pair_swap(theirs, "head", 1).astype(jnp.float32)).astype(jnp.bfloat16)
    far = pair_swap(pair, "head", 2)
    total = (pair.astype(jnp.float32) + far.astype(jnp.float32)).astype(jnp.bfloat16)
    other = pair_swap(total, "head", 1)
    first = core == 0
    return jnp.concatenate(
        [jnp.where(first, total, other), jnp.where(first, other, total)], axis=0
    ).astype(jnp.float32)


def swap_blocks(blocks, sign):
    group = lax.axis_size("ctx")
    me = lax.axis_index("ctx")
    got = [lax.dynamic_index_in_dim(blocks, me, 0, keepdims=False)]
    for k in range(1, group):
        send = lax.dynamic_index_in_dim(blocks, (me + k) % group, 0, keepdims=False)
        got.append(passed_along(send, "ctx", k))
    stacked = jnp.stack(got)
    return [
        lax.dynamic_index_in_dim(stacked, (me - j) % group, 0, keepdims=False)
        for j in range(group)
    ]


def turn(values, cosine, sine):
    half = HD // 2
    lower, upper = values[..., :half, :], values[..., half:, :]
    return jnp.concatenate(
        [lower * cosine - upper * sine, upper * cosine + lower * sine], axis=-2
    )


def tables(positions):
    frequency = theta_base ** (-(jnp.arange(HD // 2, dtype=jnp.float32) * (2.0 / HD)))
    angles = frequency[:, None] * positions.astype(jnp.float32)[None, :]
    return (jnp.cos(angles), jnp.sin(angles))


def attend_kernel(tile, span_ref, q_ref, k_ref, v_ref, row_doc_ref, col_doc_ref, out_ref, lse_ref, keys_scr):
    step = pl.program_id(0)

    @pl.when(step == 0)
    def _():
        keys_scr[...] = k_ref[...].T

    q = q_ref[...]
    doc = row_doc_ref[...]
    first, last = span_ref[0, step], span_ref[1, step]

    def body(j, state):
        top, total, out = state
        at = pl.multiple_of(j * tile, tile)
        s = jnp.dot(keys_scr[pl.ds(at, tile), :], q, preferred_element_type=jnp.float32)
        allowed = col_doc_ref[pl.ds(at, tile), :] == doc
        s = jnp.where(allowed, s, masked_score)
        new_top = jnp.maximum(top, jnp.max(s, axis=0, keepdims=True))
        e = jnp.where(allowed, jnp.exp(s - new_top), 0.0)
        factor = jnp.exp(top - new_top)
        total = total * factor + jnp.sum(e, axis=0, keepdims=True)
        out = out * factor + jnp.dot(
            v_ref[:, pl.ds(at, tile)], e.astype(jnp.bfloat16), preferred_element_type=jnp.float32
        )
        return (new_top, total, out)

    width = q.shape[1]
    state = (
        jnp.full((1, width), masked_score, jnp.float32),
        jnp.zeros((1, width), jnp.float32),
        jnp.zeros((HD, width), jnp.float32),
    )
    top, total, out = lax.fori_loop(first, last, body, state)
    out_ref[...] = out / total
    lse_ref[...] = top + jnp.log(total)


def attend_back_kernel(
    tile, span_ref, q_ref, k_ref, v_ref, row_doc_ref, col_doc_ref, lse_ref, out_ref, grad_ref,
    dq_ref, dk_ref, dv_ref, keys_scr, values_scr,
):
    step = pl.program_id(0)

    @pl.when(step == 0)
    def _():
        keys_scr[...] = k_ref[...].T
        values_scr[...] = v_ref[...].T
        dk_ref[...] = jnp.zeros_like(dk_ref)
        dv_ref[...] = jnp.zeros_like(dv_ref)

    q = q_ref[...]
    grad = grad_ref[...]
    delta = jnp.sum(grad.astype(jnp.float32) * out_ref[...], axis=0, keepdims=True)
    doc = row_doc_ref[...]
    lse = lse_ref[...]
    q_rows = q.T
    grad_rows = grad.T
    first, last = span_ref[0, step], span_ref[1, step]

    def body(j, dq):
        at = pl.multiple_of(j * tile, tile)
        s = jnp.dot(keys_scr[pl.ds(at, tile), :], q, preferred_element_type=jnp.float32)
        allowed = col_doc_ref[pl.ds(at, tile), :] == doc
        p = jnp.where(allowed, jnp.exp(s - lse), 0.0)
        dp = jnp.dot(values_scr[pl.ds(at, tile), :], grad, preferred_element_type=jnp.float32)
        ds = (p * (dp - delta)).astype(jnp.bfloat16)
        dv_ref[pl.ds(at, tile), :] += jnp.dot(
            p.astype(jnp.bfloat16), grad_rows, preferred_element_type=jnp.float32
        )
        dk_ref[pl.ds(at, tile), :] += jnp.dot(ds, q_rows, preferred_element_type=jnp.float32)
        return dq + jnp.dot(
            k_ref[:, pl.ds(at, tile)], ds, preferred_element_type=jnp.float32
        )

    dq_ref[...] = lax.fori_loop(first, last, body, jnp.zeros(q.shape, jnp.float32))


def tile_spans(lengths, tiles, tile):
    ends = jnp.cumsum(lengths, dtype=jnp.int32)
    starts = ends - lengths
    low_row = jnp.arange(tiles, dtype=jnp.int32) * tile
    high_row = low_row + (tile - 1)
    low_doc = jnp.sum((low_row[:, None] >= ends[None, :]).astype(jnp.int32), axis=1)
    high_doc = jnp.sum((high_row[:, None] >= ends[None, :]).astype(jnp.int32), axis=1)
    slots = jnp.arange(lengths.shape[0], dtype=jnp.int32)[None, :]
    begin = jnp.sum(jnp.where(slots == low_doc[:, None], starts[None, :], 0), axis=1)
    finish = jnp.sum(jnp.where(slots == high_doc[:, None], ends[None, :], 0), axis=1)
    return jnp.stack([begin // tile, (finish + (tile - 1)) // tile]).astype(jnp.int32)


def head_specs(tile, total):
    moving = pl.BlockSpec((HD, tile), lambda i, span: (0, i))
    whole = pl.BlockSpec((HD, total), lambda i, span: (0, 0))
    row = pl.BlockSpec((1, tile), lambda i, span: (0, i))
    column = pl.BlockSpec((total, 1), lambda i, span: (0, 0))
    return (moving, whole, row, column)


def attend(q, k, v, doc, spans, tile):
    total = q.shape[1]
    moving, whole, row, column = head_specs(tile, total)
    return pl.pallas_call(
        functools.partial(attend_kernel, tile),
        grid_spec=pltpu.PrefetchScalarGridSpec(
            num_scalar_prefetch=1,
            grid=(total // tile,),
            in_specs=[moving, whole, whole, row, column],
            out_specs=[moving, row],
            scratch_shapes=[pltpu.VMEM((total, HD), jnp.bfloat16)],
        ),
        out_shape=[
            jax.ShapeDtypeStruct((HD, total), jnp.float32),
            jax.ShapeDtypeStruct((1, total), jnp.float32),
        ],
        compiler_params=pltpu.CompilerParams(vmem_limit_bytes=40 * 1024 * 1024),
        cost_estimate=pl.CostEstimate(
            flops=10 * total * total * HD, bytes_accessed=4 * total * HD, transcendentals=total * total
        ),
        name="attend",
    )(spans, q, k, v, doc[None, :], doc[:, None])


def attend_back(q, k, v, doc, spans, tile, lse, out, grad):
    total = q.shape[1]
    moving, whole, row, column = head_specs(tile, total)
    tall = pl.BlockSpec((total, HD), lambda i, span: (0, 0))
    dq, dk, dv = pl.pallas_call(
        functools.partial(attend_back_kernel, tile),
        grid_spec=pltpu.PrefetchScalarGridSpec(
            num_scalar_prefetch=1,
            grid=(total // tile,),
            in_specs=[moving, whole, whole, row, column, row, moving, moving],
            out_specs=[moving, tall, tall],
            scratch_shapes=[
                pltpu.VMEM((total, HD), jnp.bfloat16),
                pltpu.VMEM((total, HD), jnp.bfloat16),
            ],
        ),
        out_shape=[
            jax.ShapeDtypeStruct((HD, total), jnp.float32),
            jax.ShapeDtypeStruct((total, HD), jnp.float32),
            jax.ShapeDtypeStruct((total, HD), jnp.float32),
        ],
        compiler_params=pltpu.CompilerParams(vmem_limit_bytes=40 * 1024 * 1024),
        cost_estimate=pl.CostEstimate(
            flops=20 * total * total * HD, bytes_accessed=4 * total * HD, transcendentals=total * total
        ),
        name="attend_back",
    )(spans, q, k, v, doc[None, :], doc[:, None], lse, out, grad)
    return (dq, dk.T, dv.T)


def per_device(tokens, doc_lengths, norm_gains, w_qkv, w_out, w_in, w_down, cotangent):
    rows = tokens.shape[1]
    hidden = tokens[0].astype(jnp.float32)
    lengths = doc_lengths[0]
    group = lax.axis_size("ctx")
    me = lax.axis_index("ctx")
    width = w_qkv.shape[2]
    heads = width // HD
    each = heads // group
    scale = HD ** (-0.5)
    gains = gather_gains(norm_gains).astype(jnp.float32)
    qkv_full = gather_weight(w_qkv, 1)
    tail_full = gather_weight(jnp.concatenate([w_out, w_down], axis=0), 1)
    out_full, down_full = (tail_full[:width], tail_full[width:])
    in_full = gather_weight(w_in, 1)
    doc_all, pos_all = token_layout(lengths, jnp.int32(0), rows * group)
    cos_all, sin_all = tables(pos_all)
    cos_here = lax.dynamic_slice_in_dim(cos_all, me * rows, rows, 1)
    sin_here = lax.dynamic_slice_in_dim(sin_all, me * rows, rows, 1)

    normed_one, inverse_one, scaled_one = layer_norm(hidden, gains[0])
    input_one = scaled_one.astype(jnp.bfloat16)
    raw = jnp.einsum("cdn,td->cnt", qkv_full, input_one, preferred_element_type=jnp.float32)
    raw = raw.reshape(3, heads, HD, rows)
    q = (turn(raw[0], cos_here, sin_here) * scale).astype(jnp.bfloat16)
    k = turn(raw[1], cos_here, sin_here).astype(jnp.bfloat16)
    v = raw[2].astype(jnp.bfloat16)
    blocks = jnp.stack([q, k, v], axis=1).reshape(group, each, 3, HD, rows)
    mine = jnp.concatenate(swap_blocks(blocks, 1), axis=-1)
    q, k, v = (mine[:, 0], mine[:, 1], mine[:, 2])
    q, k, v = (q.reshape(HD, -1), k.reshape(HD, -1), v.reshape(HD, -1))
    tile = 512 if rows * group % 512 == 0 else 128
    spans = tile_spans(lengths, rows * group // tile, tile)
    attn_float, lse = attend(q, k, v, doc_all, spans, tile)
    parts = attn_float.astype(jnp.bfloat16).reshape(each, HD, group, rows).transpose(2, 0, 1, 3)
    attn_low = jnp.concatenate(swap_blocks(parts, -1), axis=0).reshape(width, rows)

    partial_out = jnp.einsum("nt,nd->td", attn_low, out_full, preferred_element_type=jnp.float32)
    resid_one = hidden + head_sum(partial_out)
    normed_two, inverse_two, scaled_two = layer_norm(resid_one, gains[1])
    input_two = scaled_two.astype(jnp.bfloat16)
    gate_up = jnp.einsum("td,cdf->tcf", input_two, in_full, preferred_element_type=jnp.float32)
    activated, gelu_back = jax.vjp(exact_gelu, gate_up[:, 0])
    mixed_low = (activated * gate_up[:, 1]).astype(jnp.bfloat16)
    partial_ffn = jnp.dot(mixed_low, down_full, preferred_element_type=jnp.float32)

    grad_rows = cotangent[0]
    grad_mixed = jnp.einsum("td,fd->tf", grad_rows, down_full, preferred_element_type=jnp.float32)
    grad_gate = gelu_back(grad_mixed * gate_up[:, 1])[0]
    grad_up = grad_mixed * activated
    grad_gate_up = jnp.stack([grad_gate, grad_up], axis=1).astype(jnp.bfloat16)
    partial_two = jnp.einsum(
        "tcf,cdf->td", grad_gate_up, in_full, preferred_element_type=jnp.float32
    )
    grad_input_two = head_sum(partial_two)
    grad_down = jnp.einsum(
        "tf,td->df", mixed_low, grad_rows, preferred_element_type=jnp.float32
    )
    grad_in = jnp.einsum(
        "td,tcf->cdf", input_two, grad_gate_up, preferred_element_type=jnp.float32
    )
    grad_input_two, grad_down, grad_in = lax.optimization_barrier(
        (grad_input_two, grad_down.astype(jnp.bfloat16), grad_in.astype(jnp.bfloat16))
    )
    share_down = reduce_weight(grad_down[None])
    share_in = reduce_weight(grad_in)
    result = (resid_one + head_sum(partial_ffn)).astype(jnp.bfloat16)
    grad_norm_two, gain_grad_two = norm_back(grad_input_two, normed_two, inverse_two, gains[1])
    grad_resid = grad_rows.astype(jnp.float32) + grad_norm_two
    grad_branch = grad_resid.astype(jnp.bfloat16)
    grad_attn = jnp.einsum(
        "nd,td->nt", out_full, grad_branch, preferred_element_type=jnp.float32
    ).astype(jnp.bfloat16)
    grad_mine = jnp.concatenate(
        swap_blocks(grad_attn.reshape(group, each, HD, rows), 1), axis=-1
    )
    grad_out = jnp.einsum(
        "nt,td->dn", attn_low, grad_branch, preferred_element_type=jnp.float32
    )
    grad_mine, grad_out = lax.optimization_barrier((grad_mine, grad_out))
    share_out = reduce_weight(grad_out[None])
    grad_q, grad_k, grad_v = attend_back(
        q, k, v, doc_all, spans, tile, lse, attn_float, grad_mine.reshape(HD, -1)
    )
    grad_q = turn(grad_q, cos_all, -sin_all) * scale
    grad_k = turn(grad_k, cos_all, -sin_all)
    back = jnp.stack([grad_q, grad_k, grad_v]).astype(jnp.bfloat16)
    back = back.reshape(each, 3, HD, group, rows).transpose(3, 0, 1, 2, 4)
    grad_raw = jnp.concatenate(swap_blocks(back, -1), axis=0)
    grad_raw = grad_raw.transpose(1, 0, 2, 3).reshape(3, width, rows)
    partial_one = jnp.einsum(
        "cnt,cdn->td", grad_raw, qkv_full, preferred_element_type=jnp.float32
    )
    grad_qkv = jnp.einsum(
        "td,cnt->cdn", input_one, grad_raw, preferred_element_type=jnp.float32
    )
    partial_one, grad_qkv, share_down, share_in, share_out = lax.optimization_barrier(
        (partial_one, grad_qkv.astype(jnp.bfloat16), share_down, share_in, share_out)
    )
    share_qkv = reduce_weight(grad_qkv)
    grad_input_one = head_sum(partial_one)
    grad_norm_one, gain_grad_one = norm_back(grad_input_one, normed_one, inverse_one, gains[0])
    grad_tokens = (grad_resid + grad_norm_one).astype(jnp.bfloat16)
    total_gains = reduce_gains(jnp.stack([gain_grad_one, gain_grad_two]))
    return (
        result[None],
        grad_tokens[None],
        total_gains,
        reduce_weight_rows(share_qkv),
        reduce_weight_rows(share_out)[0].T,
        reduce_weight_rows(share_in),
        reduce_weight_rows(share_down)[0].T,
    )


def solution(mesh):
    heads = 1024 // HD // mesh.shape["head"]
    body = per_device if heads == mesh.shape["ctx"] else per_device_ring
    return jax.shard_map(
        body,
        mesh=mesh,
        in_specs=(
            P("seq", "ctx", None),
            P("seq", None),
            P(None, "ctx"),
            P(None, "ctx", "head"),
            P("head", "ctx"),
            P(None, "ctx", "head"),
            P("head", "ctx"),
            P("seq", "ctx", None),
        ),
        out_specs=(
            P("seq", "ctx", None),
            P("seq", "ctx", None),
            P(None, "ctx"),
            P(None, "ctx", "head"),
            P("head", "ctx"),
            P(None, "ctx", "head"),
            P("head", "ctx"),
        ),
        check_vma=False,
    )
```
